1024 devices in a mesh: lon: 32 (over z_lo, x), lat: 32 (over y, z_hi, core).
Axes of the slice: x: 4, y: 4, z: 32 (z_hi: 4, z_lo: 8; z = z_hi * 8 + z_lo), core: 2. Of those that a mesh axis runs over, the one named last changes fastest.
Arguments:
- model_variables: float32 [3, 64, 256, 4096], P(None, None, 'lat', 'lon'), may hold values from -6 to 6
- obs_cell: int32 [2, 64], replicated, may hold values from 0 to 1048575
- obs_value: float32 [2, 64], replicated, may hold values from -8 to 8
- obs_variance: float32 [2, 64], replicated, may hold values from 0.2 to 2
- tile_mask: int32 [2, 64, 1024], P(None, None, ('lon', 'lat')), may hold values 0 or 1
Outputs:
- analysis: float32 [3, 64, 256, 4096], P(None, None, 'lat', 'lon')
The draws below stay inside these ranges and needn't reach their ends.
All inputs are finite; a program needn't handle non-finite values. No bound on the sum of `tile_mask` on one device may be relied on, other than what follows from the above.
Results may differ from the reference program's by a relative error of at most 0.00015.
Values sent between devices are 32-bit elements; how exact they have to be, the bound alone decides.
A program may use at most 32 MiB of HBM per device.

```python
import math
import jax
import jax.numpy as jnp
from jax import lax

MEMBERS = 64
LAT_DEV = 8
LON_DEV = 128
STEPS = 4
NBATCH = 2
NOBS = 64
NLAT = 256
NLON = 4096
NTILES = 1024
LOC_RADIUS = 256
N_LON = 32
N_LAT = 32


def touch_ends(drawn, rng, smallest, top_value):
    place = [jax.random.randint(jax.random.fold_in(rng, axis), (), 0, length) for axis, length in enumerate(drawn.shape)]
    longest = drawn.shape.index(max(drawn.shape))
    beside = place[:longest] + [(place[longest] + 1) % drawn.shape[longest]] + place[longest + 1:]
    return drawn.at[tuple(place)].set(smallest).at[tuple(beside)].set(top_value)


def steps_of(stream_key, extent, split, low, high):
    def one(position, blocks):
        draws = jax.random.uniform(jax.random.fold_in(jax.random.fold_in(stream_key, 6), position), (blocks,), jnp.float32, low / len(split), high / len(split))
        return jnp.repeat(jnp.exp(draws), extent[position] // blocks).reshape((-1,) + (1,) * (len(extent) - position - 1))

    level = one(*split[0])
    for cut in split[1:]:
        level = level * one(*cut)
    return level


def centred(stream_key, extent, deviation, limit, cuts=(), kind=jnp.bfloat16):
    result = jax.random.normal(stream_key, extent, jnp.float32) * deviation
    if len(cuts) > 0:
        result = steps_of(stream_key, extent, cuts, -0.22, 0.18) * result
    return jnp.clip(result, min=-limit, max=limit).astype(kind)


def setup_inputs(seed: int = 0) -> dict:
    streams_of = jax.random.split(jax.random.key(seed), 6)
    model_variables = centred(streams_of[0], (3, MEMBERS, NLAT, NLON), 1.0, 6.0, ((2, 32), (3, 32)), jnp.float32)
    obs_cell = touch_ends(jax.random.randint(streams_of[1], (NBATCH, NOBS), 0, NLAT * NLON), jax.random.fold_in(streams_of[1], 1), 0, (NLAT * NLON) - 1).astype(jnp.int32)
    obs_value = centred(streams_of[2], (NBATCH, NOBS), 1.5, 8.0, (), jnp.float32)
    obs_variance = jnp.clip(jnp.exp(jax.random.uniform(streams_of[3], (NBATCH, NOBS), jnp.float32, math.log(0.2), math.log(2.0))), 0.2, 2.0)
    tile_mask = touch_ends((jax.random.randint(streams_of[4], (NBATCH, NOBS, NTILES), 0, 4) < 3).astype(jnp.int32), jax.random.fold_in(streams_of[4], 1), 0, 1)
    return dict(model_variables=model_variables, obs_cell=obs_cell, obs_value=obs_value, obs_variance=obs_variance, tile_mask=tile_mask)


CORIOLIS = 0.1
COURANT = 0.5
SMALL_EPSILON = 1e-06

def east_diff(field):
    return 0.5 * (jnp.roll(field, -1, axis=-1) - jnp.roll(field, 1, axis=-1))

def north_diff(field):
    padded = jnp.pad(field, ((1, 1), (0, 0)))
    return 0.5 * (padded[2:] - padded[:-2])

def single_prediction(layered_arrays):
    surface_elevation, east, north = (layered_arrays[0], layered_arrays[1], layered_arrays[2])
    rows = jnp.arange(NLAT, dtype=jnp.int32).astype(jnp.float32)
    coriolis = (CORIOLIS * ((2.0 * rows + 1.0) / NLAT - 1.0))[:, None]
    for step in range(STEPS):
        surface_elevation = surface_elevation - COURANT * (east_diff(east) + north_diff(north))
        east_next = east + coriolis * north - COURANT * east_diff(surface_elevation)
        north = north - coriolis * east - COURANT * north_diff(surface_elevation)
        east = east_next
    return jnp.stack([surface_elevation, east, north])

def increments(prior, value, variance):
    center = jnp.mean(prior)
    spread_dev = prior - center
    spread = jnp.sum(spread_dev * spread_dev) / (MEMBERS - 1) + SMALL_EPSILON
    post = 1.0 / (1.0 / spread + 1.0 / variance)
    post_mean = post * (center / spread + value / variance)
    delta = post_mean - center + (jnp.sqrt(post / spread) - 1.0) * spread_dev
    slope = spread_dev / ((MEMBERS - 1) * spread)
    return (delta, slope)

def tile_weights(cells, mask_batch):
    obs_lat = cells // NLON
    obs_lon = cells % NLON
    tiles = jnp.arange(N_LON * N_LAT, dtype=jnp.int32)
    centre_lat = tiles % N_LAT * LAT_DEV + LAT_DEV // 2
    central_longitude = tiles // N_LAT * LON_DEV + LON_DEV // 2
    lat_gap = obs_lat[:, None] - centre_lat[None, :]
    lon_gap = jnp.abs(obs_lon[:, None] - central_longitude[None, :])
    lon_gap = jnp.minimum(lon_gap, NLON - lon_gap)
    distance = (lat_gap * lat_gap + lon_gap * lon_gap).astype(jnp.float32)
    return mask_batch.astype(jnp.float32) / (1.0 + distance / (LOC_RADIUS * LOC_RADIUS))

def assimilate(model_variables, cells, values, variances, weights):
    surface_elevation = model_variables[0]
    obs_lat = cells // NLON
    obs_lon = cells % NLON
    priors = jnp.transpose(surface_elevation[:, obs_lat, obs_lon])
    owning_patch = obs_lon // LON_DEV * N_LAT + obs_lat // LAT_DEV
    links = jnp.transpose(weights[:, owning_patch])
    tiles = N_LON * N_LAT
    transforms = jnp.broadcast_to(jnp.eye(MEMBERS, dtype=jnp.float32), (tiles, MEMBERS, MEMBERS))

    def turn(k, carry):
        priors, transforms = carry
        delta, slope = increments(priors[k], values[k], variances[k])
        coef = links[:, k] * jnp.dot(priors, slope, precision=lax.Precision.HIGHEST)
        priors = priors + coef[:, None] * delta[None, :]
        lifted = jnp.einsum('tmn,n->tm', transforms, slope, precision=lax.Precision.HIGHEST)
        transforms = transforms + weights[k][:, None, None] * lifted[:, :, None] * delta[None, None, :]
        return (priors, transforms)
    priors, transforms = lax.fori_loop(0, NOBS, turn, (priors, transforms))
    grid = transforms.reshape(N_LON, N_LAT, MEMBERS, MEMBERS)
    tiled = model_variables.reshape(3, MEMBERS, N_LAT, LAT_DEV, N_LON, LON_DEV)
    tiled = jnp.moveaxis(tiled, 4, 0)

    def apply_column(pair):
        block, mats = pair
        return jnp.einsum('fmaij,amn->fnaij', block, mats, precision=lax.Precision.HIGHEST)
    updated = lax.map(apply_column, (tiled, grid))
    return jnp.moveaxis(updated, 0, 4).reshape(model_variables.shape)

def reference(model_variables, obs_cell, obs_value, obs_variance, tile_mask):
    ensemble_snapshots = lax.map(single_prediction, jnp.moveaxis(model_variables, 1, 0))
    model_variables = jnp.moveaxis(ensemble_snapshots, 0, 1)
    for batch in range(NBATCH):
        cells = obs_cell[batch]
        weights = tile_weights(cells, tile_mask[batch])
        model_variables = assimilate(model_variables, cells, obs_value[batch], obs_variance[batch], weights)
    return model_variables
```

```python
import functools

import jax
import jax.numpy as jnp
from jax import lax
from jax.experimental import pallas as pl
from jax.experimental.pallas import tpu as pltpu
from jax.sharding import PartitionSpec as P

MESH = pl.DeviceIdType.MESH
F32 = jnp.float32
BF16 = jnp.bfloat16

STEPS = 4
LOC_RADIUS = 256
CORIOLIS = 0.1
SMALL_EPSILON = 1e-06
MEMBERS = 64
ROWS = 8
COLS = 128
GROUPS = 8
HALVES = 2 * STEPS
EXT = HALVES - 1
PICK_ROWS = ROWS + 2 * EXT


class Geometry:
    def __init__(self, n_lon, n_lat):
        self.n_lon, self.n_lat = n_lon, n_lat
        if (n_lon, n_lat) == (32, 32):
            self.x, self.y, self.zh, self.c = 4, 4, 4, 2
        else:
            self.x, self.y, self.zh, self.c = 1, 1, n_lat // 2, 2
        self.zl = n_lon // self.x
        self.near = self.x * self.y * self.c
        self.far = self.zl * self.zh
        self.total_rows = ROWS * n_lat
        self.total_cols = COLS * n_lon

    def near_index(self, lon, lat):
        return (lon % self.x) * (self.y * self.c) + (lat // (self.zh * self.c)) * self.c + lat % self.c

    def near_peer(self, i, lon, lat):
        x, y, c = i // (self.y * self.c), (i // self.c) % self.y, i % self.c
        return (lon // self.x) * self.x + x, (y * self.zh + (lat // self.c) % self.zh) * self.c + c

    def far_index(self, lon, lat):
        return ((lat // self.c) % self.zh) * self.zl + lon // self.x

    def far_peer(self, i, lon, lat):
        zh, zl = i // self.zl, i % self.zl
        return zl * self.x + lon % self.x, ((lat // (self.zh * self.c)) * self.zh + zh) * self.c + lat % self.c


def iota(shape, dim):
    return lax.broadcasted_iota(jnp.int32, shape, dim)


def roll(v, shift):
    return pltpu.roll(v, shift % COLS, 1)


def pack_edges(tiles):
    lane = iota((8, COLS), 1)
    out = None
    for s, t in enumerate(tiles):
        r = roll(t, 16 * s + 8)
        out = r if out is None else jnp.where(lane // 16 == s, r, out)
    return out


def unpack_edges(packed, s):
    return roll(packed, -(16 * s + 8))


def lon_diff(m, s, first, last):
    mp, sp, mm, sm = roll(m, -1), roll(s, -1), roll(m, 1), roll(s, 1)
    return (
        jnp.where(last, sp, mp) - jnp.where(first, sm, mm),
        jnp.where(last, mp, sp) - jnp.where(first, mm, sm),
    )


def column_of(row, eye):
    return jnp.sum(jnp.where(eye, row, 0.0), axis=1, keepdims=True)


class Sum:
    def __init__(self, geo, lon, lat, refs, sems):
        self.geo, self.lon, self.lat = geo, lon, lat
        self.src, self.near, self.mid, self.far, self.last, self.out = refs
        self.sems = sems
        self.me = geo.near_index(lon, lat)
        self.me_far = geo.far_index(lon, lat)

    def _send(self, stage, src, dst, n, me, peer):
        def one(i, carry):
            p = lax.rem(me + i, n)
            pltpu.make_async_remote_copy(
                src_ref=src(p),
                dst_ref=dst.at[me],
                send_sem=self.sems.at[0, stage],
                recv_sem=self.sems.at[1, stage],
                device_id=peer(p, self.lon, self.lat),
                device_id_type=MESH,
            ).start()
            return carry

        lax.fori_loop(1, n, one, 0)

    def _wait(self, stage, buf, n):
        if n > 1:
            part = buf.at[pl.ds(0, n - 1)]
            pltpu.make_async_copy(part, part, self.sems.at[1, stage]).wait()

    def _added(self, buf, n):
        total = buf[0]
        for i in range(1, n):
            total = total + buf[i]
        return total

    def send_near(self):
        self.near[self.me] = self.src[self.me]
        self._send(0, lambda p: self.src.at[p], self.near, self.geo.near, self.me, self.geo.near_peer)

    def send_far(self):
        self._wait(0, self.near, self.geo.near)
        total = self._added(self.near, self.geo.near)
        self.mid[...] = total
        self.far[self.me_far] = total
        self._send(1, lambda p: self.mid, self.far, self.geo.far, self.me_far, self.geo.far_peer)

    def send_last(self):
        self._wait(1, self.far, self.geo.far)
        total = self._added(self.far, self.geo.far)
        self.last[...] = total
        self.out[self.me] = total
        self._send(2, lambda p: self.last, self.out, self.geo.near, self.me, self.geo.near_peer)

    def wait_last(self):
        self._wait(2, self.out, self.geo.near)

    def wait_sends(self):
        for stage, buf, n in ((0, self.near, self.geo.near), (1, self.far, self.geo.far), (2, self.out, self.geo.near)):
            if n > 1:
                part = buf.at[pl.ds(0, n - 1)]
                pltpu.make_async_copy(part, part, self.sems.at[0, stage]).wait()


def forecast_kernel(
    geo, x_ref, cell_ref, value_ref, variance_ref, mask_ref,
    f_ref, c_ref, y_ref,
    main, side, edges, edges_in, series, series_in, ghosts, heights, onehot,
    l0, l1, l2, l3, l4, l5, p0, p1, p2, p3, p4, p5,
    lon_sems, lat_sems, l_sems, p_sems,
):
    lon, lat = lax.axis_index("lon"), lax.axis_index("lat")
    n_lon, n_lat = geo.n_lon, geo.n_lat
    east, west = lax.rem(lon + 1, n_lon), lax.rem(lon + n_lon - 1, n_lon)
    after, before = lax.rem(lat + 1, n_lat), lax.rem(lat + n_lat - 1, n_lat)
    links = Sum(geo, lon, lat, (l0, l1, l2, l3, l4, l5), l_sems)
    priors = Sum(geo, lon, lat, (p0, p1, p2, p3, p4, p5), p_sems)

    barrier = pltpu.get_barrier_semaphore()
    for d in ((east, lat), (west, lat), (lon, after), (lon, before)):
        pl.semaphore_signal(barrier, inc=1, device_id=d, device_id_type=MESH)

    def greet(n, me, peer):
        def one(i, carry):
            pl.semaphore_signal(barrier, inc=1, device_id=peer(lax.rem(me + i, n), lon, lat), device_id_type=MESH)
            return carry

        lax.fori_loop(1, n, one, 0)

    greet(geo.far, links.me_far, geo.far_peer)
    greet(geo.near, links.me, geo.near_peer)

    row_first, col_first = lat * ROWS, lon * COLS

    def field_row(f, g, r):
        return x_ref[f, pl.ds(g * 64 + r, 8, stride=8), :]

    def pack(g, carry):
        for f in range(3):
            edges[g, f] = pack_edges([field_row(f, g, r) for r in range(ROWS)])
        return carry

    lax.fori_loop(0, GROUPS, pack, 0)

    lane = iota((8, COLS), 1)
    first, last = lane == 0, lane == COLS - 1
    big_row, big_col = iota((128, 128), 0), iota((128, 128), 1)
    eye = big_row == big_col
    cells = jnp.concatenate([cell_ref[0:1, :], cell_ref[1:2, :]], axis=1)
    obs_row, obs_col = cells // geo.total_cols, cells % geo.total_cols
    match_col = big_row + col_first == obs_col
    for i in range(PICK_ROWS):
        hit = match_col & (obs_row == row_first + (i - EXT))
        onehot[i * 128:(i + 1) * 128, :] = jnp.where(hit, 1.0, 0.0).astype(BF16)
    owned = jnp.where((obs_row // ROWS == lat) & (obs_col // COLS == lon), 1.0, 0.0)
    mask_col = mask_ref[...].astype(F32)
    share = mask_col * owned
    per = 128 // geo.near
    for i in range(geo.near):
        l0[i] = share[i * per:(i + 1) * per, :]
    cells_col = column_of(cells.astype(F32), eye).astype(jnp.int32)
    row_col, col_col = cells_col // geo.total_cols, cells_col % geo.total_cols

    def damping(centre_row, centre_col):
        row_gap = row_col - centre_row
        col_gap = jnp.abs(col_col - centre_col)
        col_gap = jnp.minimum(col_gap, geo.total_cols - col_gap)
        distance = (row_gap * row_gap + col_gap * col_gap).astype(F32)
        return 1.0 + distance / (LOC_RADIUS * LOC_RADIUS)

    own = mask_col / damping(row_first + ROWS // 2, col_first + COLS // 2)
    value_col = column_of(jnp.concatenate([value_ref[0:1, :], value_ref[1:2, :]], axis=1), eye)
    variance_col = column_of(jnp.concatenate([variance_ref[0:1, :], variance_ref[1:2, :]], axis=1), eye)
    c_ref[1] = jnp.broadcast_to(1.0 / variance_col, (128, 128))
    c_ref[2] = jnp.broadcast_to(value_col, (128, 128))
    c_ref[3] = jnp.broadcast_to(own, (128, 128))

    pl.semaphore_wait(barrier, 4 + (geo.far - 1) + (geo.near - 1))

    def lon_copies(g):
        return [
            pltpu.make_async_remote_copy(
                src_ref=edges.at[g], dst_ref=edges_in.at[s, g], send_sem=lon_sems.at[0, s, g], recv_sem=lon_sems.at[1, s, g],
                device_id=(d, lat), device_id_type=MESH,
            )
            for s, d in ((0, east), (1, west))
        ]

    def lat_copies(g):
        return [
            pltpu.make_async_remote_copy(
                src_ref=series.at[s, g], dst_ref=series_in.at[1 - s, g], send_sem=lat_sems.at[0, s, g],
                recv_sem=lat_sems.at[1, 1 - s, g], device_id=(lon, d), device_id_type=MESH,
            )
            for s, d in ((0, before), (1, after))
        ]

    def start_lon(g, carry):
        for c in lon_copies(g):
            c.start()
        return carry

    lax.fori_loop(0, GROUPS, start_lon, 0)
    links.send_near()

    has_before = jnp.where(lat > 0, 1.0, 0.0)
    has_after = jnp.where(lat < n_lat - 1, 1.0, 0.0)

    def turning(r):
        row = (row_first + r).astype(F32)
        return CORIOLIS * ((2.0 * row + 1.0) / geo.total_rows - 1.0)

    def fit(r, v):
        return v * has_before if r < 0 else v * has_after if r >= ROWS else v

    class State:
        def __init__(self, g):
            self.rows = [set(range(ROWS)) for _ in range(3)]
            from_west = lane % 16 < 8
            for f in range(3):
                packed = jnp.where(from_west, edges_in[0, g, f], edges_in[1, g, f])
                for r in range(ROWS):
                    main[f, r + 8] = field_row(f, g, r)
                    side[f, r + 8] = unpack_edges(packed, r)

        def get(self, f, r):
            if r not in self.rows[f]:
                return None
            return main[f, r + 8], side[f, r + 8]

        def put(self, f, r, v):
            self.rows[f].add(r)
            main[f, r + 8], side[f, r + 8] = v

    def less(a, b):
        if a is None and b is None:
            return None
        if b is None:
            return a
        if a is None:
            return tuple(-q for q in b)
        return tuple(p - q for p, q in zip(a, b))

    def plus(a, b):
        if a is None or b is None:
            return a if b is None else b
        return tuple(p + q for p, q in zip(a, b))

    def scaled(a, k):
        return None if a is None else tuple(p * k for p in a)

    def lon_of(v):
        return None if v is None else lon_diff(v[0], v[1], first, last)

    def half_step(st, p, lo, hi, ghost=None):
        at = (lambda f, r: ghost[r] if ghost is not None and r in ghost else st.get(f, r))
        for r in range(lo, hi):
            if p % 2:
                slope = plus(lon_of(st.get(1, r)), less(at(2, r + 1), at(2, r - 1)))
                new = less(st.get(0, r), scaled(slope, 0.25))
                st.put(0, r, tuple(fit(r, v) for v in new))
            else:
                e, n, k = st.get(1, r), st.get(2, r), turning(r)
                new_e = less(plus(e, scaled(n, k)), scaled(lon_of(st.get(0, r)), 0.25))
                new_n = less(less(n, scaled(e, k)), scaled(less(at(0, r + 1), at(0, r - 1)), 0.25))
                if new_e is not None:
                    st.put(1, r, tuple(fit(r, v) for v in new_e))
                if new_n is not None:
                    st.put(2, r, tuple(fit(r, v) for v in new_n))

    def spread(g, carry):
        for c in lon_copies(g):
            c.wait_recv()
        st = State(g)
        sides = ([], [])
        for p in range(HALVES):
            if p > 0:
                half_step(st, p, -p, ROWS + p)
            f = 0 if p % 2 else 2
            for s, (r, outside) in enumerate(((0, -1), (ROWS - 1, ROWS))):
                m, e = st.get(f, r)
                series[s, g, p] = m
                sides[s].append(e)
                if p > 0:
                    ghosts[g, s, p, 0], ghosts[g, s, p, 1] = st.get(f, outside)
        for s in range(2):
            series[s, g, HALVES] = pack_edges(sides[s])
        for c in lat_copies(g):
            c.start()
        for i in range(PICK_ROWS):
            heights[pl.ds(pl.multiple_of(g * 8, 8), 8), i * 128:(i + 1) * 128] = main[0, i - EXT + 8]
        return carry

    lax.fori_loop(0, GROUPS, spread, 0)

    total = jnp.zeros((3 * MEMBERS, 128), F32)
    for i in range(PICK_ROWS // 2):
        v = heights[:, i * 256:(i + 1) * 256]
        high = v.astype(BF16)
        rest = v - high.astype(F32)
        middle = rest.astype(BF16)
        low = (rest - middle.astype(F32)).astype(BF16)
        total = total + jnp.dot(
            jnp.concatenate([high, middle, low], axis=0), onehot[i * 256:(i + 1) * 256, :], preferred_element_type=F32
        )
    picked = total[:MEMBERS] + (total[MEMBERS:2 * MEMBERS] + total[2 * MEMBERS:])
    few = MEMBERS // geo.near
    for i in range(geo.near):
        p0[i] = picked[i * few:(i + 1) * few, :]
    priors.send_near()
    links.send_far()
    priors.send_far()

    def settle(g, carry):
        for c in lat_copies(g):
            c.wait_recv()
        st = State(g)
        packed = [series_in[s, g, HALVES] for s in range(2)]
        for p in range(1, HALVES + 1):
            ghost = {}
            for s, (outside, there) in enumerate(((-1, has_before), (ROWS, has_after))):
                v = (series_in[s, g, p - 1] * there, unpack_edges(packed[s], p - 1) * there)
                if p > 1:
                    v = plus(v, (ghosts[g, s, p - 1, 0], ghosts[g, s, p - 1, 1]))
                ghost[outside] = v
            half_step(st, p, 0, ROWS, ghost)
        for f in range(3):
            for r in range(ROWS):
                f_ref[f * ROWS + r, pl.ds(pl.multiple_of(g * 8, 8), 8), :] = main[f, r + 8]
        return carry

    lax.fori_loop(0, 2, settle, 0)
    links.send_last()
    priors.send_last()
    links.wait_last()
    for i in range(geo.near):
        c_ref[0, i * per:(i + 1) * per, :] = l5[i]
    weighted = c_ref[0] / damping(obs_row // ROWS * ROWS + ROWS // 2, obs_col // COLS * COLS + COLS // 2)
    c_ref[0] = weighted
    beside = jnp.sum(jnp.where(big_col == big_row + 1, weighted, 0.0), axis=1, keepdims=True)
    c_ref[4] = jnp.broadcast_to(beside, (128, 128))
    lax.fori_loop(2, GROUPS, settle, 0)
    priors.wait_last()
    for i in range(geo.near):
        y_ref[i * few:(i + 1) * few, :] = p5[i]

    links.wait_sends()
    priors.wait_sends()

    def finish(g, carry):
        for c in lon_copies(g) + lat_copies(g):
            c.wait_send()
        return carry

    lax.fori_loop(0, GROUPS, finish, 0)


def added_sublanes(v):
    t = v.reshape(8, 8, COLS).sum(axis=0)
    for s in (4, 2, 1):
        t = t + pltpu.roll(t, s, 0)
    return t


def tall(v):
    return jnp.concatenate([v] * 8, axis=0)


def across(column):
    return jnp.broadcast_to(column, (column.shape[0], COLS))


def update_kernel(n_obs, f_ref, c_ref, y_ref, out_ref):
    y = y_ref[...]
    mean = added_sublanes(y) * (1.0 / MEMBERS)
    b = y - tall(mean)
    a = jnp.where(iota((MEMBERS, COLS), 0) == iota((MEMBERS, COLS), 1), 1.0, 0.0)
    a_mean = jnp.zeros((8, COLS), F32)
    left = iota((8, COLS), 1) < MEMBERS

    def row(i, k):
        return jnp.broadcast_to(c_ref[i, k:k + 1, :], (8, COLS))

    d, m = across(b[:, 0:1]), across(mean[:, 0:1])
    for k in range(2 * n_obs):
        if k == n_obs:
            a, a_mean = jnp.where(tall(left), a, b), jnp.where(left, a_mean, mean)
        later = k >= n_obs
        obs, obs_mean = (a, a_mean) if later else (b, mean)
        if k + 1 < 2 * n_obs:
            d_next, m_next = across(obs[:, k + 1:k + 2]), across(obs_mean[:, k + 1:k + 2])
        s = added_sublanes(d * d) * (1.0 / (MEMBERS - 1)) + SMALL_EPSILON
        ratio = s * row(1, k)
        root = lax.rsqrt(1.0 + ratio)
        gain = root - 1.0
        shift = ratio * (root * root) * (row(2, k) - m)
        scale = 1.0 / ((MEMBERS - 1) * s)
        if k + 1 < 2 * n_obs:
            c = row(4, k) * scale * added_sublanes(d_next * d)
            new_d, new_m = d_next + tall(c * gain) * d, m_next + c * shift
        link, own = row(0, k), row(3, k)
        c = (jnp.where(left, own, link) if later else own) * scale * added_sublanes(a * d)
        a, a_mean = a + tall(c * gain) * d, a_mean + c * shift
        if not later:
            c = link * scale * added_sublanes(b * d)
            b, mean = b + tall(c * gain) * d, mean + c * shift
        if k + 1 < 2 * n_obs:
            d, m = new_d, new_m
    t = (a + tall(a_mean))[:, :MEMBERS]
    t_high = t.astype(BF16)
    t_low = (t - t_high.astype(F32)).astype(BF16)
    lhs = jnp.concatenate([t_high, t_high, t_low, t_low], axis=1)
    for i in range(0, 3 * ROWS, 2):
        v = jnp.concatenate([f_ref[i], f_ref[i + 1]], axis=1)
        high = v.astype(BF16)
        low = (v - high.astype(F32)).astype(BF16)
        r = jnp.dot(lhs, jnp.concatenate([high, low, high, low], axis=0), preferred_element_type=F32)
        for q in range(2):
            out_ref[(i + q) // ROWS, pl.ds((i + q) % ROWS, MEMBERS, stride=ROWS), :] = r[:, q * COLS:(q + 1) * COLS]


def body(geo, model_variables, obs_cell, obs_value, obs_variance, tile_mask):
    vmem = pl.BlockSpec(memory_space=pltpu.VMEM)
    x = model_variables.reshape(3, MEMBERS * ROWS, COLS)
    mask = tile_mask.reshape(128, 1)
    n, few, per = geo.near, MEMBERS // geo.near, 128 // geo.near

    def sum_buffers(rows):
        v = functools.partial(pltpu.VMEM, dtype=F32)
        return [
            v((n, rows, 128)), v((n, rows, 128)), v((rows, 128)), v((geo.far, rows, 128)), v((rows, 128)), v((n, rows, 128)),
        ]

    dma = pltpu.SemaphoreType.DMA
    f, c, y = pl.pallas_call(
        functools.partial(forecast_kernel, geo),
        out_shape=(
            jax.ShapeDtypeStruct((3 * ROWS, MEMBERS, COLS), F32),
            jax.ShapeDtypeStruct((5, 128, 128), F32),
            jax.ShapeDtypeStruct((MEMBERS, 128), F32),
        ),
        in_specs=[vmem] * 5,
        out_specs=(vmem, vmem, vmem),
        scratch_shapes=[
            pltpu.VMEM((3, 24, 8, COLS), F32),
            pltpu.VMEM((3, 24, 8, COLS), F32),
            pltpu.VMEM((GROUPS, 3, 8, COLS), F32),
            pltpu.VMEM((2, GROUPS, 3, 8, COLS), F32),
            pltpu.VMEM((2, GROUPS, HALVES + 1, 8, COLS), F32),
            pltpu.VMEM((2, GROUPS, HALVES + 1, 8, COLS), F32),
            pltpu.VMEM((GROUPS, 2, HALVES, 2, 8, COLS), F32),
            pltpu.VMEM((MEMBERS, PICK_ROWS * COLS), F32),
            pltpu.VMEM((PICK_ROWS * COLS, 128), BF16),
            *sum_buffers(per),
            *sum_buffers(few),
            dma((2, 2, GROUPS)), dma((2, 2, GROUPS)), dma((2, 3)), dma((2, 3)),
        ],
        compiler_params=pltpu.CompilerParams(collective_id=0, has_side_effects=True, vmem_limit_bytes=40 * 2**20),
    )(x, obs_cell, obs_value, obs_variance, mask)
    out = pl.pallas_call(
        functools.partial(update_kernel, obs_cell.shape[1]),
        out_shape=jax.ShapeDtypeStruct((3, MEMBERS * ROWS, COLS), F32),
        in_specs=[vmem] * 3,
        out_specs=vmem,
        compiler_params=pltpu.CompilerParams(vmem_limit_bytes=32 * 2**20),
    )(f, c, y)
    return out.reshape(3, MEMBERS, ROWS, COLS)


def solution(mesh):
    geo = Geometry(mesh.shape["lon"], mesh.shape["lat"])
    in_specs = (P(None, None, "lat", "lon"), P(), P(), P(), P(None, None, ("lon", "lat")))
    out_specs = P(None, None, "lat", "lon")
    return jax.shard_map(
        functools.partial(body, geo), mesh=mesh, in_specs=in_specs, out_specs=out_specs, check_vma=False
    )
```

```python
import functools

import jax
import jax.numpy as jnp
from jax import lax
from jax.experimental import pallas as pl
from jax.experimental.pallas import tpu as pltpu
from jax.sharding import PartitionSpec as P

MESH = pl.DeviceIdType.MESH
F32 = jnp.float32
BF16 = jnp.bfloat16

STEPS = 4
LOC_RADIUS = 256
CORIOLIS = 0.1
SMALL_EPSILON = 1e-06
MEMBERS = 64
ROWS = 8
COLS = 128
GROUPS = 8
HALVES = 2 * STEPS
EXT = HALVES - 1
PICK_ROWS = ROWS + 2 * EXT


class Geometry:
    def __init__(self, n_lon, n_lat):
        self.n_lon, self.n_lat = n_lon, n_lat
        if (n_lon, n_lat) == (32, 32):
            self.x, self.y, self.zh, self.c = 4, 4, 4, 2
        else:
            self.x, self.y, self.zh, self.c = 1, 1, n_lat // 2, 2
        self.zl = n_lon // self.x
        self.near = self.x * self.y * self.c
        self.total_rows = ROWS * n_lat
        self.total_cols = COLS * n_lon

    def near_index(self, lon, lat):
        return (lon % self.x) * (self.y * self.c) + (lat // (self.zh * self.c)) * self.c + lat % self.c

    def near_peer(self, i, lon, lat):
        x, y, c = i // (self.y * self.c), (i // self.c) % self.y, i % self.c
        return (lon // self.x) * self.x + x, (y * self.zh + (lat // self.c) % self.zh) * self.c + c


def iota(shape, dim):
    return lax.broadcasted_iota(jnp.int32, shape, dim)


def roll(v, shift):
    return pltpu.roll(v, shift % COLS, 1)


def pack_edges(tiles):
    lane = iota((8, COLS), 1)
    out = None
    for s, t in enumerate(tiles):
        r = roll(t, 16 * s + 8)
        out = r if out is None else jnp.where(lane // 16 == s, r, out)
    return out


def unpack_edges(packed, s):
    return roll(packed, -(16 * s + 8))


def lon_diff(m, s, first, last):
    mp, sp, mm, sm = roll(m, -1), roll(s, -1), roll(m, 1), roll(s, 1)
    return (
        jnp.where(last, sp, mp) - jnp.where(first, sm, mm),
        jnp.where(last, mp, sp) - jnp.where(first, mm, sm),
    )


def column_of(row, eye):
    return jnp.sum(jnp.where(eye, row, 0.0), axis=1, keepdims=True)


class Sum:
    def __init__(self, geo, lon, lat, refs, sems):
        self.geo, self.lon, self.lat = geo, lon, lat
        self.src, self.near, self.mid, self.run, self.pair, self.pair_in, self.last, self.out = refs
        self.sems = sems
        self.me = geo.near_index(lon, lat)
        self.me_run = lon // geo.x

    def run_peer(self, i, lon, lat):
        return i * self.geo.x + lon % self.geo.x, lat

    def partner(self, step):
        geo, c = self.geo, self.geo.c
        zh = (self.lat // c) % geo.zh
        up = (zh + step) % 2 == 0
        other = jnp.where(up, zh + 1, zh + geo.zh - 1) % geo.zh
        return self.lon, ((self.lat // (geo.zh * c)) * geo.zh + other) * c + self.lat % c

    def _send(self, stage, src, dst, n, me, peer):
        def one(i, carry):
            p = lax.rem(me + i, n)
            pltpu.make_async_remote_copy(
                src_ref=src(p),
                dst_ref=dst.at[me],
                send_sem=self.sems.at[0, stage],
                recv_sem=self.sems.at[1, stage],
                device_id=peer(p, self.lon, self.lat),
                device_id_type=MESH,
            ).start()
            return carry

        lax.fori_loop(1, n, one, 0)

    def _wait(self, stage, buf, n, side=1):
        part = buf.at[pl.ds(0, n - 1)]
        pltpu.make_async_copy(part, part, self.sems.at[side, stage]).wait()

    def _added(self, buf, n):
        total = buf[0]
        for i in range(1, n):
            total = total + buf[i]
        return total

    def _pair_copy(self, step):
        return pltpu.make_async_remote_copy(
            src_ref=self.pair.at[step], dst_ref=self.pair_in.at[step], send_sem=self.sems.at[0, 2 + step],
            recv_sem=self.sems.at[1, 2 + step], device_id=self.partner(step), device_id_type=MESH,
        )

    def send_near(self):
        self.near[self.me] = self.src[self.me]
        self._send(0, lambda p: self.src.at[p], self.near, self.geo.near, self.me, self.geo.near_peer)

    def send_run(self):
        self._wait(0, self.near, self.geo.near)
        total = self._added(self.near, self.geo.near)
        self.mid[...] = total
        self.run[self.me_run] = total
        self._send(1, lambda p: self.mid, self.run, self.geo.zl, self.me_run, self.run_peer)

    def send_pair(self):
        self._wait(1, self.run, self.geo.zl)
        self.pair[0] = self._added(self.run, self.geo.zl)
        self._pair_copy(0).start()

    def send_pairs(self):
        self._pair_copy(0).wait_recv()
        self.pair[1] = self.pair[0] + self.pair_in[0]
        self._pair_copy(1).start()

    def send_last(self):
        self._pair_copy(1).wait_recv()
        total = self.pair[1] + self.pair_in[1]
        self.last[...] = total
        self.out[self.me] = total
        self._send(4, lambda p: self.last, self.out, self.geo.near, self.me, self.geo.near_peer)

    def wait_last(self):
        self._wait(4, self.out, self.geo.near)

    def wait_sends(self):
        for stage, buf, n in ((0, self.near, self.geo.near), (1, self.run, self.geo.zl), (4, self.out, self.geo.near)):
            self._wait(stage, buf, n, side=0)
        for step in range(2):
            self._pair_copy(step).wait_send()


def forecast_kernel(
    geo, x_hbm, cell_hbm, value_hbm, variance_hbm, mask_hbm,
    f_ref, c_ref, y_ref,
    x_ref, cell_ref, value_ref, variance_ref, mask_ref, main, side, edges, edges_in, series, series_in, late, late_in, ghosts, heights, onehot,
    s0, s1, s2, s3, s4, s5, s6, s7,
    in_sems, lon_sems, lat_sems, late_sems, sum_sems,
):
    lon, lat = lax.axis_index("lon"), lax.axis_index("lat")
    n_lon, n_lat = geo.n_lon, geo.n_lat
    east, west = lax.rem(lon + 1, n_lon), lax.rem(lon + n_lon - 1, n_lon)
    after, before = lax.rem(lat + 1, n_lat), lax.rem(lat + n_lat - 1, n_lat)
    shared = Sum(geo, lon, lat, (s0, s1, s2, s3, s4, s5, s6, s7), sum_sems)

    loads = [
        pltpu.make_async_copy(src, dst, in_sems.at[i])
        for i, (src, dst) in enumerate(
            (
                (x_hbm, x_ref), (cell_hbm, cell_ref), (value_hbm, value_ref), (variance_hbm, variance_ref), (mask_hbm, mask_ref),
            )
        )
    ]
    for load in loads:
        load.start()
    barrier = pltpu.get_barrier_semaphore()

    def greet(n, me, peer):
        def one(i, carry):
            pl.semaphore_signal(barrier, inc=1, device_id=peer(lax.rem(me + i, n), lon, lat), device_id_type=MESH)
            return carry

        lax.fori_loop(1, n, one, 0)

    for d in ((lon, after), (lon, before), shared.partner(0), shared.partner(1), (east, lat), (west, lat)):
        pl.semaphore_signal(barrier, inc=1, device_id=d, device_id_type=MESH)
    greet(geo.zl, shared.me_run, shared.run_peer)
    greet(geo.near, shared.me, geo.near_peer)

    row_first, col_first = lat * ROWS, lon * COLS
    lane = iota((8, COLS), 1)
    first, last = lane == 0, lane == COLS - 1
    edge = (lane < 8) | (lane >= COLS - 8)
    nothing = jnp.zeros((8, COLS), F32)
    has_before = jnp.where(lat > 0, 1.0, 0.0)
    has_after = jnp.where(lat < n_lat - 1, 1.0, 0.0)

    def field_row(f, g, r):
        return x_ref[f, pl.ds(g * 64 + r, 8, stride=8), :]

    def turning(r):
        row = (row_first + r).astype(F32)
        return CORIOLIS * ((2.0 * row + 1.0) / geo.total_rows - 1.0)

    def fit(r, v):
        return v * has_before if r < 0 else v * has_after if r >= ROWS else v

    class State:
        def __init__(self, g, own, sides):
            self.rows = [set(range(ROWS)) for _ in range(3)]
            for f in range(3):
                if sides:
                    packed = jnp.where(lane % 16 < 8, edges_in[0, g, f], edges_in[1, g, f])
                for r in range(ROWS):
                    main[f, r + 8] = field_row(f, g, r) if own else nothing
                    side[f, r + 8] = unpack_edges(packed, r) if sides else nothing

        def get(self, f, r):
            if r not in self.rows[f]:
                return None
            return main[f, r + 8], side[f, r + 8]

        def put(self, f, r, v):
            self.rows[f].add(r)
            main[f, r + 8], side[f, r + 8] = v

    def less(a, b):
        if a is None and b is None:
            return None
        if b is None:
            return a
        if a is None:
            return tuple(-q for q in b)
        return tuple(p - q for p, q in zip(a, b))

    def plus(a, b):
        if a is None or b is None:
            return a if b is None else b
        return tuple(p + q for p, q in zip(a, b))

    def scaled(a, k):
        return None if a is None else tuple(p * k for p in a)

    def lon_of(v):
        return None if v is None else lon_diff(v[0], v[1], first, last)

    def half_step(st, p, rows, ghost=None):
        at = (lambda f, r: ghost[r] if ghost is not None and r in ghost else st.get(f, r))
        for r in rows:
            if p % 2:
                slope = plus(lon_of(st.get(1, r)), less(at(2, r + 1), at(2, r - 1)))
                new = less(st.get(0, r), scaled(slope, 0.25))
                st.put(0, r, tuple(fit(r, v) for v in new))
            else:
                e, n, k = st.get(1, r), st.get(2, r), turning(r)
                new_e = less(plus(e, scaled(n, k)), scaled(lon_of(st.get(0, r)), 0.25))
                new_n = less(less(n, scaled(e, k)), scaled(less(at(0, r + 1), at(0, r - 1)), 0.25))
                if new_e is not None:
                    st.put(1, r, tuple(fit(r, v) for v in new_e))
                if new_n is not None:
                    st.put(2, r, tuple(fit(r, v) for v in new_n))

    beside = ((0, -1), (ROWS - 1, ROWS))

    def spread_tile(g, carry):
        for f in range(3):
            edges[g, f] = pack_edges([field_row(f, g, r) for r in range(ROWS)])
        st = State(g, True, False)
        sides = ([], [])
        for p in range(HALVES):
            if p > 0:
                half_step(st, p, range(-p, ROWS + p))
            f = 0 if p % 2 else 2
            for s, (r, outside) in enumerate(beside):
                m, e = st.get(f, r)
                series[s, g, p] = m
                sides[s].append(e)
                if p > 0:
                    ghosts[g, s, p, 0], ghosts[g, s, p, 1] = st.get(f, outside)
        for s in range(2):
            late[s, g, 0] = pack_edges(sides[s])
        here = pl.ds(pl.multiple_of(g * 8, 8), 8)
        for i in range(PICK_ROWS):
            heights[here, i * 128:(i + 1) * 128] = main[0, i - EXT + 8]
        for q in range(3):
            tiles = [side[0, i - EXT + 8] if i < PICK_ROWS else nothing for i in range(8 * q, 8 * q + 8)]
            heights[here, (PICK_ROWS + q) * 128:(PICK_ROWS + q + 1) * 128] = pack_edges(tiles)
        heights[here, (PICK_ROWS + 3) * 128:] = nothing
        return carry

    for load in loads:
        load.wait()
    lax.fori_loop(0, GROUPS, spread_tile, 0)

    big_row, big_col = iota((128, 128), 0), iota((128, 128), 1)
    eye = big_row == big_col
    cells = jnp.concatenate([cell_ref[0:1, :], cell_ref[1:2, :]], axis=1)
    obs_row, obs_col = cells // geo.total_cols, cells % geo.total_cols
    match_col = big_row + col_first == obs_col
    for i in range(PICK_ROWS):
        hit = match_col & (obs_row == row_first + (i - EXT))
        onehot[i * 128:(i + 1) * 128, :] = jnp.where(hit, 1.0, 0.0).astype(BF16)
    within = big_row % 16
    side_col = (jnp.where(within < 8, col_first - 8 + within, col_first + 120 + within) + geo.total_cols) % geo.total_cols
    match_col = side_col == obs_col
    for q in range(3):
        hit = match_col & (obs_row == row_first + (8 * q - EXT) + big_row // 16)
        i = PICK_ROWS + q
        onehot[i * 128:(i + 1) * 128, :] = jnp.where(hit, 1.0, 0.0).astype(BF16)
    onehot[(PICK_ROWS + 3) * 128:, :] = jnp.zeros((128, 128), BF16)
    total = jnp.zeros((3 * MEMBERS, 128), F32)
    for i in range((PICK_ROWS + 4) // 2):
        v = heights[:, i * 256:(i + 1) * 256]
        high = v.astype(BF16)
        rest = v - high.astype(F32)
        middle = rest.astype(BF16)
        low = (rest - middle.astype(F32)).astype(BF16)
        total = total + jnp.dot(
            jnp.concatenate([high, middle, low], axis=0), onehot[i * 256:(i + 1) * 256, :], preferred_element_type=F32
        )
    picked = total[:MEMBERS] + (total[MEMBERS:2 * MEMBERS] + total[2 * MEMBERS:])
    few, per = MEMBERS // geo.near, 128 // geo.near
    owned = jnp.where((obs_row // ROWS == lat) & (obs_col // COLS == lon), 1.0, 0.0)
    mask_row = jnp.concatenate([mask_ref[0], mask_ref[1]], axis=1).astype(F32)
    mask_col = column_of(mask_row, eye)
    share = mask_col * owned
    for i in range(geo.near):
        s0[i, 0:few, :] = picked[i * few:(i + 1) * few, :]
        s0[i, few:few + per, :] = share[i * per:(i + 1) * per, :]
        s0[i, few + per:, :] = jnp.zeros((s0.shape[1] - few - per, 128), F32)

    def lon_copies(g):
        return [
            pltpu.make_async_remote_copy(
                src_ref=edges.at[g], dst_ref=edges_in.at[s, g], send_sem=lon_sems.at[0, s, g], recv_sem=lon_sems.at[1, s, g],
                device_id=(d, lat), device_id_type=MESH,
            )
            for s, d in ((0, east), (1, west))
        ]

    def lat_copies(g, src, dst, sems):
        return [
            pltpu.make_async_remote_copy(
                src_ref=src.at[s, g], dst_ref=dst.at[1 - s, g], send_sem=sems.at[0, s, g],
                recv_sem=sems.at[1, 1 - s, g], device_id=(lon, d), device_id_type=MESH,
            )
            for s, d in ((0, before), (1, after))
        ]

    def series_copies(g):
        return lat_copies(g, series, series_in, lat_sems)

    def late_copies(g):
        return lat_copies(g, late, late_in, late_sems)

    def start(copies, lo, hi):
        def one(g, carry):
            for c in copies(g):
                c.start()
            return carry

        lax.fori_loop(lo, hi, one, 0)

    pl.semaphore_wait(barrier, 6 + (geo.zl - 1) + (geo.near - 1))
    shared.send_near()
    start(lon_copies, 0, GROUPS)
    start(series_copies, 0, 2)

    cells_col = column_of(cells.astype(F32), eye).astype(jnp.int32)
    row_col, col_col = cells_col // geo.total_cols, cells_col % geo.total_cols

    def damping(centre_row, centre_col):
        row_gap = row_col - centre_row
        col_gap = jnp.abs(col_col - centre_col)
        col_gap = jnp.minimum(col_gap, geo.total_cols - col_gap)
        distance = (row_gap * row_gap + col_gap * col_gap).astype(F32)
        return 1.0 + distance / (LOC_RADIUS * LOC_RADIUS)

    own = mask_col / damping(row_first + ROWS // 2, col_first + COLS // 2)
    value_col = column_of(jnp.concatenate([value_ref[0:1, :], value_ref[1:2, :]], axis=1), eye)
    variance_col = column_of(jnp.concatenate([variance_ref[0:1, :], variance_ref[1:2, :]], axis=1), eye)
    c_ref[1] = jnp.broadcast_to(1.0 / variance_col, (128, 128))
    c_ref[2] = jnp.broadcast_to(value_col, (128, 128))
    c_ref[3] = jnp.broadcast_to(own, (128, 128))

    shared.send_run()
    start(series_copies, 2, 4)

    def spread_sides(g, carry):
        for c in lon_copies(g):
            c.wait_recv()
        st = State(g, False, True)
        sides, mains = ([], []), ([], [])
        for p in range(HALVES):
            if p > 0:
                reach = EXT - p
                rows = [
                    r for r in range(-p, ROWS + p)
                    if -1 - reach <= r <= reach or ROWS - 1 - reach <= r <= ROWS + reach
                ]
                half_step(st, p, rows)
            f = 0 if p % 2 else 2
            for s, (r, outside) in enumerate(beside):
                m, e = st.get(f, r)
                mains[s].append(m)
                sides[s].append(e)
                if p > 0:
                    m, e = st.get(f, outside)
                    ghosts[g, s, p, 0] += m
                    ghosts[g, s, p, 1] += e
        for s in range(2):
            late[s, g, 0] += pack_edges(sides[s])
            late[s, g, 1] = pack_edges(mains[s])
        return carry

    def settle(g, carry):
        for c in series_copies(g) + late_copies(g):
            c.wait_recv()
        st = State(g, True, True)
        packed = [(late_in[s, g, 0], late_in[s, g, 1]) for s in range(2)]
        for p in range(1, HALVES + 1):
            ghost = {}
            for s, ((_, outside), there) in enumerate(zip(beside, (has_before, has_after))):
                m = series_in[s, g, p - 1] + jnp.where(edge, unpack_edges(packed[s][1], p - 1), 0.0)
                v = (m * there, unpack_edges(packed[s][0], p - 1) * there)
                if p > 1:
                    v = plus(v, (ghosts[g, s, p - 1, 0], ghosts[g, s, p - 1, 1]))
                ghost[outside] = v
            half_step(st, p, range(ROWS), ghost)
        for f in range(3):
            for r in range(ROWS):
                f_ref[f * ROWS + r, pl.ds(pl.multiple_of(g * 8, 8), 8), :] = main[f, r + 8]
        return carry

    lax.fori_loop(0, GROUPS, spread_sides, 0)
    shared.send_pair()
    start(late_copies, 0, 4)
    start(series_copies, 4, 7)
    shared.send_pairs()
    start(series_copies, 7, GROUPS)
    start(late_copies, 4, GROUPS)
    lax.fori_loop(0, 2, settle, 0)
    shared.send_last()

    lax.fori_loop(2, GROUPS, settle, 0)
    shared.wait_last()
    for i in range(geo.near):
        y_ref[i * few:(i + 1) * few, :] = s7[i, 0:few, :]
        c_ref[0, i * per:(i + 1) * per, :] = s7[i, few:few + per, :]
    weighted = c_ref[0] / damping(obs_row // ROWS * ROWS + ROWS // 2, obs_col // COLS * COLS + COLS // 2)
    c_ref[0] = weighted
    following = jnp.sum(jnp.where(big_col == big_row + 1, weighted, 0.0), axis=1, keepdims=True)
    c_ref[4] = jnp.broadcast_to(following, (128, 128))

    shared.wait_sends()

    def finish(g, carry):
        for c in lon_copies(g) + series_copies(g) + late_copies(g):
            c.wait_send()
        return carry

    lax.fori_loop(0, GROUPS, finish, 0)


def added_sublanes(v):
    t = v.reshape(8, 8, COLS).sum(axis=0)
    for s in (4, 2, 1):
        t = t + pltpu.roll(t, s, 0)
    return t


def tall(v):
    return jnp.concatenate([v] * 8, axis=0)


def across(column):
    return jnp.broadcast_to(column, (column.shape[0], COLS))


def update_kernel(n_obs, f_ref, c_ref, y_ref, out_ref):
    y = y_ref[...]
    mean = added_sublanes(y) * (1.0 / MEMBERS)
    b = y - tall(mean)
    a = jnp.where(iota((MEMBERS, COLS), 0) == iota((MEMBERS, COLS), 1), 1.0, 0.0)
    a_mean = jnp.zeros((8, COLS), F32)
    left = iota((8, COLS), 1) < MEMBERS

    def row(i, k):
        return jnp.broadcast_to(c_ref[i, k:k + 1, :], (8, COLS))

    d, m = across(b[:, 0:1]), across(mean[:, 0:1])
    for k in range(2 * n_obs):
        if k == n_obs:
            a, a_mean = jnp.where(tall(left), a, b), jnp.where(left, a_mean, mean)
        later = k >= n_obs
        obs, obs_mean = (a, a_mean) if later else (b, mean)
        if k + 1 < 2 * n_obs:
            d_next, m_next = across(obs[:, k + 1:k + 2]), across(obs_mean[:, k + 1:k + 2])
        s = added_sublanes(d * d) * (1.0 / (MEMBERS - 1)) + SMALL_EPSILON
        ratio = s * row(1, k)
        root = lax.rsqrt(1.0 + ratio)
        gain = root - 1.0
        shift = ratio * (root * root) * (row(2, k) - m)
        scale = 1.0 / ((MEMBERS - 1) * s)
        if k + 1 < 2 * n_obs:
            c = row(4, k) * scale * added_sublanes(d_next * d)
            new_d, new_m = d_next + tall(c * gain) * d, m_next + c * shift
        link, own = row(0, k), row(3, k)
        c = (jnp.where(left, own, link) if later else own) * scale * added_sublanes(a * d)
        a, a_mean = a + tall(c * gain) * d, a_mean + c * shift
        if not later:
            c = link * scale * added_sublanes(b * d)
            b, mean = b + tall(c * gain) * d, mean + c * shift
        if k + 1 < 2 * n_obs:
            d, m = new_d, new_m
    t = (a + tall(a_mean))[:, :MEMBERS]
    t_high = t.astype(BF16)
    t_low = (t - t_high.astype(F32)).astype(BF16)
    lhs = jnp.concatenate([t_high, t_high, t_low, t_low], axis=1)
    for i in range(0, 3 * ROWS, 2):
        v = jnp.concatenate([f_ref[i], f_ref[i + 1]], axis=1)
        high = v.astype(BF16)
        low = (v - high.astype(F32)).astype(BF16)
        r = jnp.dot(lhs, jnp.concatenate([high, low, high, low], axis=0), preferred_element_type=F32)
        for q in range(2):
            out_ref[(i + q) // ROWS, pl.ds((i + q) % ROWS, MEMBERS, stride=ROWS), :] = r[:, q * COLS:(q + 1) * COLS]


def body(geo, model_variables, obs_cell, obs_value, obs_variance, tile_mask):
    vmem = pl.BlockSpec(memory_space=pltpu.VMEM)
    x = model_variables.reshape(3, MEMBERS * ROWS, COLS)
    mask = jnp.transpose(tile_mask, (0, 2, 1))
    n, rows = geo.near, -(-(MEMBERS + 128) // geo.near // 8) * 8
    dma = pltpu.SemaphoreType.DMA

    def v(*shape, dtype=F32):
        return pltpu.VMEM(shape, dtype)

    f, c, y = pl.pallas_call(
        functools.partial(forecast_kernel, geo),
        out_shape=(
            jax.ShapeDtypeStruct((3 * ROWS, MEMBERS, COLS), F32),
            jax.ShapeDtypeStruct((5, 128, 128), F32),
            jax.ShapeDtypeStruct((MEMBERS, 128), F32),
        ),
        in_specs=[pl.BlockSpec(memory_space=pltpu.HBM)] * 5,
        out_specs=(vmem, vmem, vmem),
        scratch_shapes=[
            v(3, MEMBERS * ROWS, COLS),
            v(*obs_cell.shape, dtype=jnp.int32), v(*obs_value.shape), v(*obs_value.shape), v(*mask.shape, dtype=jnp.int32),
            v(3, 24, 8, COLS),
            v(3, 24, 8, COLS),
            v(GROUPS, 3, 8, COLS),
            v(2, GROUPS, 3, 8, COLS),
            v(2, GROUPS, HALVES, 8, COLS),
            v(2, GROUPS, HALVES, 8, COLS),
            v(2, GROUPS, 2, 8, COLS),
            v(2, GROUPS, 2, 8, COLS),
            v(GROUPS, 2, HALVES, 2, 8, COLS),
            v(MEMBERS, (PICK_ROWS + 4) * COLS),
            v((PICK_ROWS + 4) * COLS, 128, dtype=BF16),
            v(n, rows, 128), v(n, rows, 128), v(rows, 128), v(geo.zl, rows, 128), v(2, rows, 128), v(2, rows, 128), v(rows, 128),
            v(n, rows, 128),
            dma((5,)), dma((2, 2, GROUPS)), dma((2, 2, GROUPS)), dma((2, 2, GROUPS)), dma((2, 5)),
        ],
        compiler_params=pltpu.CompilerParams(collective_id=0, has_side_effects=True, vmem_limit_bytes=40 * 2**20),
    )(x, obs_cell, obs_value, obs_variance, mask)
    out = pl.pallas_call(
        functools.partial(update_kernel, obs_cell.shape[1]),
        out_shape=jax.ShapeDtypeStruct((3, MEMBERS * ROWS, COLS), F32),
        in_specs=[vmem] * 3,
        out_specs=vmem,
        compiler_params=pltpu.CompilerParams(vmem_limit_bytes=32 * 2**20),
    )(f, c, y)
    return out.reshape(3, MEMBERS, ROWS, COLS)


def solution(mesh):
    geo = Geometry(mesh.shape["lon"], mesh.shape["lat"])
    in_specs = (P(None, None, "lat", "lon"), P(), P(), P(), P(None, None, ("lon", "lat")))
    out_specs = P(None, None, "lat", "lon")
    return jax.shard_map(
        functools.partial(body, geo), mesh=mesh, in_specs=in_specs, out_specs=out_specs, check_vma=False
    )
```

```python
import functools

import jax
import jax.numpy as jnp
from jax import lax
from jax.experimental import pallas as pl
from jax.experimental.pallas import tpu as pltpu
from jax.sharding import PartitionSpec as P

MESH = pl.DeviceIdType.MESH
F32 = jnp.float32
BF16 = jnp.bfloat16

STEPS = 4
LOC_RADIUS = 256
CORIOLIS = 0.1
SMALL_EPSILON = 1e-06
MEMBERS = 64
ROWS = 8
COLS = 128
GROUPS = 8
HALVES = 2 * STEPS
EXT = HALVES - 1
PICK_ROWS = ROWS + 2 * EXT


class Geometry:
    def __init__(self, n_lon, n_lat):
        self.n_lon, self.n_lat = n_lon, n_lat
        if (n_lon, n_lat) == (32, 32):
            self.x, self.y, self.zh, self.c = 4, 4, 4, 2
        else:
            self.x, self.y, self.zh, self.c = 1, 1, n_lat // 2, 2
        self.zl = n_lon // self.x
        self.near = self.x * self.y * self.c
        self.total_rows = ROWS * n_lat
        self.total_cols = COLS * n_lon

    def near_index(self, lon, lat):
        return (lon % self.x) * (self.y * self.c) + (lat // (self.zh * self.c)) * self.c + lat % self.c

    def near_peer(self, i, lon, lat):
        x, y, c = i // (self.y * self.c), (i // self.c) % self.y, i % self.c
        return (lon // self.x) * self.x + x, (y * self.zh + (lat // self.c) % self.zh) * self.c + c


def iota(shape, dim):
    return lax.broadcasted_iota(jnp.int32, shape, dim)


def roll(v, shift):
    return pltpu.roll(v, shift % COLS, 1)


def pack_edges(tiles):
    lane = iota((8, COLS), 1)
    out = None
    for s, t in enumerate(tiles):
        r = roll(t, 16 * s + 8)
        out = r if out is None else jnp.where(lane // 16 == s, r, out)
    return out


def unpack_edges(packed, s):
    return roll(packed, -(16 * s + 8))


def lon_diff(m, s, first, last):
    mp, sp, mm, sm = roll(m, -1), roll(s, -1), roll(m, 1), roll(s, 1)
    return (
        jnp.where(last, sp, mp) - jnp.where(first, sm, mm),
        jnp.where(last, mp, sp) - jnp.where(first, mm, sm),
    )


def column_of(row, eye):
    return jnp.sum(jnp.where(eye, row, 0.0), axis=1, keepdims=True)


class Sum:
    def __init__(self, geo, lon, lat, refs, sems):
        self.geo, self.lon, self.lat = geo, lon, lat
        self.src, self.near, self.mid, self.run, self.pair, self.pair_in, self.last, self.out = refs
        self.sems = sems
        self.me = geo.near_index(lon, lat)
        self.me_run = lon // geo.x

    def run_peer(self, i, lon, lat):
        return i * self.geo.x + lon % self.geo.x, lat

    def partner(self, step):
        geo, c = self.geo, self.geo.c
        zh = (self.lat // c) % geo.zh
        up = (zh + step) % 2 == 0
        other = jnp.where(up, zh + 1, zh + geo.zh - 1) % geo.zh
        return self.lon, ((self.lat // (geo.zh * c)) * geo.zh + other) * c + self.lat % c

    def _send(self, stage, src, dst, n, me, peer):
        def one(i, carry):
            p = lax.rem(me + i, n)
            pltpu.make_async_remote_copy(
                src_ref=src(p),
                dst_ref=dst.at[me],
                send_sem=self.sems.at[0, stage],
                recv_sem=self.sems.at[1, stage],
                device_id=peer(p, self.lon, self.lat),
                device_id_type=MESH,
            ).start()
            return carry

        lax.fori_loop(1, n, one, 0)

    def _wait(self, stage, buf, n, side=1):
        part = buf.at[pl.ds(0, n - 1)]
        pltpu.make_async_copy(part, part, self.sems.at[side, stage]).wait()

    def _added(self, buf, n):
        total = buf[0]
        for i in range(1, n):
            total = total + buf[i]
        return total

    def _pair_copy(self, step):
        return pltpu.make_async_remote_copy(
            src_ref=self.pair.at[step], dst_ref=self.pair_in.at[step], send_sem=self.sems.at[0, 2 + step],
            recv_sem=self.sems.at[1, 2 + step], device_id=self.partner(step), device_id_type=MESH,
        )

    def send_near(self):
        self.near[self.me] = self.src[self.me]
        self._send(0, lambda p: self.src.at[p], self.near, self.geo.near, self.me, self.geo.near_peer)

    def send_run(self):
        self._wait(0, self.near, self.geo.near)
        total = self._added(self.near, self.geo.near)
        self.mid[...] = total
        self.run[self.me_run] = total
        self._send(1, lambda p: self.mid, self.run, self.geo.zl, self.me_run, self.run_peer)

    def send_pair(self):
        self._wait(1, self.run, self.geo.zl)
        self.pair[0] = self._added(self.run, self.geo.zl)
        self._pair_copy(0).start()

    def send_pairs(self):
        self._pair_copy(0).wait_recv()
        self.pair[1] = self.pair[0] + self.pair_in[0]
        self._pair_copy(1).start()

    def send_last(self):
        self._pair_copy(1).wait_recv()
        total = self.pair[1] + self.pair_in[1]
        self.last[...] = total
        self.out[self.me] = total
        self._send(4, lambda p: self.last, self.out, self.geo.near, self.me, self.geo.near_peer)

    def wait_last(self):
        self._wait(4, self.out, self.geo.near)

    def wait_sends(self):
        for stage, buf, n in ((0, self.near, self.geo.near), (1, self.run, self.geo.zl), (4, self.out, self.geo.near)):
            self._wait(stage, buf, n, side=0)
        for step in range(2):
            self._pair_copy(step).wait_send()


def forecast_kernel(
    geo, x_hbm, cell_hbm, value_hbm, variance_hbm, mask_hbm,
    f_ref, c_ref, y_ref,
    x_ref, cell_ref, value_ref, variance_ref, mask_ref, main, side, edges, edges_in, series, series_in, late, late_in, ghosts, heights, onehot,
    s0, s1, s2, s3, s4, s5, s6, s7,
    in_sems, lon_sems, lat_sems, late_sems, sum_sems,
):
    lon, lat = lax.axis_index("lon"), lax.axis_index("lat")
    n_lon, n_lat = geo.n_lon, geo.n_lat
    east, west = lax.rem(lon + 1, n_lon), lax.rem(lon + n_lon - 1, n_lon)
    after, before = lax.rem(lat + 1, n_lat), lax.rem(lat + n_lat - 1, n_lat)
    shared = Sum(geo, lon, lat, (s0, s1, s2, s3, s4, s5, s6, s7), sum_sems)

    loads = [
        pltpu.make_async_copy(src, dst, in_sems.at[i])
        for i, (src, dst) in enumerate(
            (
                (x_hbm, x_ref), (cell_hbm, cell_ref), (value_hbm, value_ref), (variance_hbm, variance_ref), (mask_hbm, mask_ref),
            )
        )
    ]
    for load in loads:
        load.start()
    barrier = pltpu.get_barrier_semaphore()

    def greet(n, me, peer):
        def one(i, carry):
            pl.semaphore_signal(barrier, inc=1, device_id=peer(lax.rem(me + i, n), lon, lat), device_id_type=MESH)
            return carry

        lax.fori_loop(1, n, one, 0)

    for d in ((lon, after), (lon, before), shared.partner(0), shared.partner(1), (east, lat), (west, lat)):
        pl.semaphore_signal(barrier, inc=1, device_id=d, device_id_type=MESH)
    greet(geo.zl, shared.me_run, shared.run_peer)
    greet(geo.near, shared.me, geo.near_peer)

    row_first, col_first = lat * ROWS, lon * COLS
    lane = iota((8, COLS), 1)
    first, last = lane == 0, lane == COLS - 1
    edge = (lane < 8) | (lane >= COLS - 8)
    nothing = jnp.zeros((8, COLS), F32)
    has_before = jnp.where(lat > 0, 1.0, 0.0)
    has_after = jnp.where(lat < n_lat - 1, 1.0, 0.0)

    def field_row(f, g, r):
        return x_ref[f, pl.ds(g * 64 + r, 8, stride=8), :]

    def turning(r):
        row = (row_first + r).astype(F32)
        return CORIOLIS * ((2.0 * row + 1.0) / geo.total_rows - 1.0)

    def fit(r, v):
        return v * has_before if r < 0 else v * has_after if r >= ROWS else v

    class State:
        def __init__(self, g, own, sides):
            self.rows = [set(range(ROWS)) for _ in range(3)]
            for f in range(3):
                if sides:
                    packed = jnp.where(lane % 16 < 8, edges_in[0, g, f], edges_in[1, g, f])
                for r in range(ROWS):
                    main[f, r + 8] = field_row(f, g, r) if own else nothing
                    side[f, r + 8] = unpack_edges(packed, r) if sides else nothing

        def get(self, f, r):
            if r not in self.rows[f]:
                return None
            return main[f, r + 8], side[f, r + 8]

        def put(self, f, r, v):
            self.rows[f].add(r)
            main[f, r + 8], side[f, r + 8] = v

    def less(a, b):
        if a is None and b is None:
            return None
        if b is None:
            return a
        if a is None:
            return tuple(-q for q in b)
        return tuple(p - q for p, q in zip(a, b))

    def plus(a, b):
        if a is None or b is None:
            return a if b is None else b
        return tuple(p + q for p, q in zip(a, b))

    def scaled(a, k):
        return None if a is None else tuple(p * k for p in a)

    def lon_of(v):
        return None if v is None else lon_diff(v[0], v[1], first, last)

    def half_step(st, p, rows, ghost=None):
        at = (lambda f, r: ghost[r] if ghost is not None and r in ghost else st.get(f, r))
        for r in rows:
            if p % 2:
                slope = plus(lon_of(st.get(1, r)), less(at(2, r + 1), at(2, r - 1)))
                new = less(st.get(0, r), scaled(slope, 0.25))
                st.put(0, r, tuple(fit(r, v) for v in new))
            else:
                e, n, k = st.get(1, r), st.get(2, r), turning(r)
                new_e = less(plus(e, scaled(n, k)), scaled(lon_of(st.get(0, r)), 0.25))
                new_n = less(less(n, scaled(e, k)), scaled(less(at(0, r + 1), at(0, r - 1)), 0.25))
                if new_e is not None:
                    st.put(1, r, tuple(fit(r, v) for v in new_e))
                if new_n is not None:
                    st.put(2, r, tuple(fit(r, v) for v in new_n))

    beside = ((0, -1), (ROWS - 1, ROWS))

    def spread_tile(g, carry):
        for f in range(3):
            edges[g, f] = pack_edges([field_row(f, g, r) for r in range(ROWS)])
        st = State(g, True, False)
        sides = ([], [])
        for p in range(HALVES):
            if p > 0:
                half_step(st, p, range(-p, ROWS + p))
            f = 0 if p % 2 else 2
            for s, (r, outside) in enumerate(beside):
                m, e = st.get(f, r)
                series[s, g, p] = m
                sides[s].append(e)
                if p > 0:
                    ghosts[g, s, p, 0], ghosts[g, s, p, 1] = st.get(f, outside)
        for s in range(2):
            late[s, g, 0] = pack_edges(sides[s])
        here = pl.ds(pl.multiple_of(g * 8, 8), 8)
        for i in range(PICK_ROWS):
            heights[here, i * 128:(i + 1) * 128] = main[0, i - EXT + 8]
        for q in range(3):
            tiles = [side[0, i - EXT + 8] if i < PICK_ROWS else nothing for i in range(8 * q, 8 * q + 8)]
            heights[here, (PICK_ROWS + q) * 128:(PICK_ROWS + q + 1) * 128] = pack_edges(tiles)
        heights[here, (PICK_ROWS + 3) * 128:] = nothing
        return carry

    for load in loads:
        load.wait()
    lax.fori_loop(0, GROUPS, spread_tile, 0)

    big_row, big_col = iota((128, 128), 0), iota((128, 128), 1)
    eye = big_row == big_col
    cells = jnp.concatenate([cell_ref[0:1, :], cell_ref[1:2, :]], axis=1)
    obs_row, obs_col = cells // geo.total_cols, cells % geo.total_cols
    match_col = big_row + col_first == obs_col
    for i in range(PICK_ROWS):
        hit = match_col & (obs_row == row_first + (i - EXT))
        onehot[i * 128:(i + 1) * 128, :] = jnp.where(hit, 1.0, 0.0).astype(BF16)
    within = big_row % 16
    side_col = (jnp.where(within < 8, col_first - 8 + within, col_first + 120 + within) + geo.total_cols) % geo.total_cols
    match_col = side_col == obs_col
    for q in range(3):
        hit = match_col & (obs_row == row_first + (8 * q - EXT) + big_row // 16)
        i = PICK_ROWS + q
        onehot[i * 128:(i + 1) * 128, :] = jnp.where(hit, 1.0, 0.0).astype(BF16)
    onehot[(PICK_ROWS + 3) * 128:, :] = jnp.zeros((128, 128), BF16)
    total = jnp.zeros((3 * MEMBERS, 128), F32)
    for i in range((PICK_ROWS + 4) // 2):
        v = heights[:, i * 256:(i + 1) * 256]
        high = v.astype(BF16)
        rest = v - high.astype(F32)
        middle = rest.astype(BF16)
        low = (rest - middle.astype(F32)).astype(BF16)
        total = total + jnp.dot(
            jnp.concatenate([high, middle, low], axis=0), onehot[i * 256:(i + 1) * 256, :], preferred_element_type=F32
        )
    picked = total[:MEMBERS] + (total[MEMBERS:2 * MEMBERS] + total[2 * MEMBERS:])
    few, per = MEMBERS // geo.near, 128 // geo.near
    owned = jnp.where((obs_row // ROWS == lat) & (obs_col // COLS == lon), 1.0, 0.0)
    mask_row = jnp.concatenate([mask_ref[0], mask_ref[1]], axis=1).astype(F32)
    mask_col = column_of(mask_row, eye)
    share = mask_col * owned
    for i in range(geo.near):
        s0[i, 0:few, :] = picked[i * few:(i + 1) * few, :]
        s0[i, few:few + per, :] = share[i * per:(i + 1) * per, :]
        s0[i, few + per:, :] = jnp.zeros((s0.shape[1] - few - per, 128), F32)

    def lon_copies(g):
        return [
            pltpu.make_async_remote_copy(
                src_ref=edges.at[g], dst_ref=edges_in.at[s, g], send_sem=lon_sems.at[0, s, g], recv_sem=lon_sems.at[1, s, g],
                device_id=(d, lat), device_id_type=MESH,
            )
            for s, d in ((0, east), (1, west))
        ]

    def lat_copies(g, src, dst, sems):
        return [
            pltpu.make_async_remote_copy(
                src_ref=src.at[s, g], dst_ref=dst.at[1 - s, g], send_sem=sems.at[0, s, g],
                recv_sem=sems.at[1, 1 - s, g], device_id=(lon, d), device_id_type=MESH,
            )
            for s, d in ((0, before), (1, after))
        ]

    def series_copies(g):
        return lat_copies(g, series, series_in, lat_sems)

    def late_copies(g):
        return lat_copies(g, late, late_in, late_sems)

    def start(copies, lo, hi):
        def one(g, carry):
            for c in copies(g):
                c.start()
            return carry

        lax.fori_loop(lo, hi, one, 0)

    pl.semaphore_wait(barrier, 6 + (geo.zl - 1) + (geo.near - 1))
    shared.send_near()
    start(lon_copies, 0, GROUPS)
    start(series_copies, 0, 2)

    cells_col = column_of(cells.astype(F32), eye).astype(jnp.int32)
    row_col, col_col = cells_col // geo.total_cols, cells_col % geo.total_cols

    def damping(centre_row, centre_col):
        row_gap = row_col - centre_row
        col_gap = jnp.abs(col_col - centre_col)
        col_gap = jnp.minimum(col_gap, geo.total_cols - col_gap)
        distance = (row_gap * row_gap + col_gap * col_gap).astype(F32)
        return 1.0 + distance / (LOC_RADIUS * LOC_RADIUS)

    c_ref[0] = damping(obs_row // ROWS * ROWS + ROWS // 2, obs_col // COLS * COLS + COLS // 2)
    own = mask_col / damping(row_first + ROWS // 2, col_first + COLS // 2)
    value_col = column_of(jnp.concatenate([value_ref[0:1, :], value_ref[1:2, :]], axis=1), eye)
    variance_col = column_of(jnp.concatenate([variance_ref[0:1, :], variance_ref[1:2, :]], axis=1), eye)
    c_ref[1] = jnp.broadcast_to(1.0 / variance_col, (128, 128))
    c_ref[2] = jnp.broadcast_to(value_col, (128, 128))
    c_ref[3] = jnp.broadcast_to(own, (128, 128))

    shared.send_run()
    start(series_copies, 2, 4)

    def spread_sides(g, carry):
        for c in lon_copies(g):
            c.wait_recv()
        st = State(g, False, True)
        sides, mains = ([], []), ([], [])
        for p in range(HALVES):
            if p > 0:
                reach = EXT - p
                rows = [
                    r for r in range(-p, ROWS + p)
                    if -1 - reach <= r <= reach or ROWS - 1 - reach <= r <= ROWS + reach
                ]
                half_step(st, p, rows)
            f = 0 if p % 2 else 2
            for s, (r, outside) in enumerate(beside):
                m, e = st.get(f, r)
                mains[s].append(m)
                sides[s].append(e)
                if p > 0:
                    m, e = st.get(f, outside)
                    ghosts[g, s, p, 0] += m
                    ghosts[g, s, p, 1] += e
        for s in range(2):
            late[s, g, 0] += pack_edges(sides[s])
            late[s, g, 1] = pack_edges(mains[s])
        return carry

    def settle(g, carry):
        for c in series_copies(g) + late_copies(g):
            c.wait_recv()
        st = State(g, True, True)
        packed = [(late_in[s, g, 0], late_in[s, g, 1]) for s in range(2)]
        for p in range(1, HALVES + 1):
            ghost = {}
            for s, ((_, outside), there) in enumerate(zip(beside, (has_before, has_after))):
                m = series_in[s, g, p - 1] + jnp.where(edge, unpack_edges(packed[s][1], p - 1), 0.0)
                v = (m * there, unpack_edges(packed[s][0], p - 1) * there)
                if p > 1:
                    v = plus(v, (ghosts[g, s, p - 1, 0], ghosts[g, s, p - 1, 1]))
                ghost[outside] = v
            half_step(st, p, range(ROWS), ghost)
        for f in range(3):
            for r in range(ROWS):
                f_ref[f * ROWS + r, pl.ds(pl.multiple_of(g * 8, 8), 8), :] = main[f, r + 8]
        return carry

    lax.fori_loop(0, 5, spread_sides, 0)
    shared.send_pair()
    start(series_copies, 4, 6)
    lax.fori_loop(5, GROUPS, spread_sides, 0)
    start(late_copies, 0, 4)
    shared.send_pairs()
    start(series_copies, 6, GROUPS)
    start(late_copies, 4, GROUPS)
    lax.fori_loop(0, 2, settle, 0)
    shared.send_last()

    lax.fori_loop(2, GROUPS, settle, 0)
    shared.wait_last()
    for i in range(geo.near):
        y_ref[i * few:(i + 1) * few, :] = s7[i, 0:few, :]
        here = slice(i * per, (i + 1) * per)
        c_ref[0, here, :] = s7[i, few:few + per, :] / c_ref[0, here, :]
    weighted = c_ref[0]
    following = jnp.sum(jnp.where(big_col == big_row + 1, weighted, 0.0), axis=1, keepdims=True)
    c_ref[4] = jnp.broadcast_to(following, (128, 128))

    shared.wait_sends()

    def finish(g, carry):
        for c in lon_copies(g) + series_copies(g) + late_copies(g):
            c.wait_send()
        return carry

    lax.fori_loop(0, GROUPS, finish, 0)


def added_sublanes(v):
    t = v.reshape(8, 8, COLS).sum(axis=0)
    for s in (4, 2, 1):
        t = t + pltpu.roll(t, s, 0)
    return t


def tall(v):
    return jnp.concatenate([v] * 8, axis=0)


def across(column):
    return jnp.broadcast_to(column, (column.shape[0], COLS))


def update_kernel(n_obs, f_ref, c_ref, y_ref, out_ref):
    y = y_ref[...]
    mean = added_sublanes(y) * (1.0 / MEMBERS)
    b = y - tall(mean)
    a = jnp.where(iota((MEMBERS, COLS), 0) == iota((MEMBERS, COLS), 1), 1.0, 0.0)
    a_mean = jnp.zeros((8, COLS), F32)
    left = iota((8, COLS), 1) < MEMBERS

    def row(i, k):
        return jnp.broadcast_to(c_ref[i, k:k + 1, :], (8, COLS))

    d, m = across(b[:, 0:1]), across(mean[:, 0:1])
    for k in range(2 * n_obs):
        if k == n_obs:
            a, a_mean = jnp.where(tall(left), a, b), jnp.where(left, a_mean, mean)
        later = k >= n_obs
        obs, obs_mean = (a, a_mean) if later else (b, mean)
        if k + 1 < 2 * n_obs:
            d_next, m_next = across(obs[:, k + 1:k + 2]), across(obs_mean[:, k + 1:k + 2])
        s = added_sublanes(d * d) * (1.0 / (MEMBERS - 1)) + SMALL_EPSILON
        ratio = s * row(1, k)
        root = lax.rsqrt(1.0 + ratio)
        gain = root - 1.0
        shift = ratio * (root * root) * (row(2, k) - m)
        scale = 1.0 / ((MEMBERS - 1) * s)
        if k + 1 < 2 * n_obs:
            c = row(4, k) * scale * added_sublanes(d_next * d)
            new_d, new_m = d_next + tall(c * gain) * d, m_next + c * shift
        link, own = row(0, k), row(3, k)
        c = (jnp.where(left, own, link) if later else own) * scale * added_sublanes(a * d)
        a, a_mean = a + tall(c * gain) * d, a_mean + c * shift
        if not later:
            c = link * scale * added_sublanes(b * d)
            b, mean = b + tall(c * gain) * d, mean + c * shift
        if k + 1 < 2 * n_obs:
            d, m = new_d, new_m
    t = (a + tall(a_mean))[:, :MEMBERS]
    t_high = t.astype(BF16)
    t_low = (t - t_high.astype(F32)).astype(BF16)
    lhs = jnp.concatenate([t_high, t_high, t_low, t_low], axis=1)
    for i in range(0, 3 * ROWS, 2):
        v = jnp.concatenate([f_ref[i], f_ref[i + 1]], axis=1)
        high = v.astype(BF16)
        low = (v - high.astype(F32)).astype(BF16)
        r = jnp.dot(lhs, jnp.concatenate([high, low, high, low], axis=0), preferred_element_type=F32)
        for q in range(2):
            out_ref[(i + q) // ROWS, pl.ds((i + q) % ROWS, MEMBERS, stride=ROWS), :] = r[:, q * COLS:(q + 1) * COLS]


def body(geo, model_variables, obs_cell, obs_value, obs_variance, tile_mask):
    vmem = pl.BlockSpec(memory_space=pltpu.VMEM)
    x = model_variables.reshape(3, MEMBERS * ROWS, COLS)
    mask = jnp.transpose(tile_mask, (0, 2, 1))
    n, rows = geo.near, -(-(MEMBERS + 128) // geo.near // 8) * 8
    dma = pltpu.SemaphoreType.DMA

    def v(*shape, dtype=F32):
        return pltpu.VMEM(shape, dtype)

    f, c, y = pl.pallas_call(
        functools.partial(forecast_kernel, geo),
        out_shape=(
            jax.ShapeDtypeStruct((3 * ROWS, MEMBERS, COLS), F32),
            jax.ShapeDtypeStruct((5, 128, 128), F32),
            jax.ShapeDtypeStruct((MEMBERS, 128), F32),
        ),
        in_specs=[pl.BlockSpec(memory_space=pltpu.HBM)] * 5,
        out_specs=(vmem, vmem, vmem),
        scratch_shapes=[
            v(3, MEMBERS * ROWS, COLS),
            v(*obs_cell.shape, dtype=jnp.int32), v(*obs_value.shape), v(*obs_value.shape), v(*mask.shape, dtype=jnp.int32),
            v(3, 24, 8, COLS),
            v(3, 24, 8, COLS),
            v(GROUPS, 3, 8, COLS),
            v(2, GROUPS, 3, 8, COLS),
            v(2, GROUPS, HALVES, 8, COLS),
            v(2, GROUPS, HALVES, 8, COLS),
            v(2, GROUPS, 2, 8, COLS),
            v(2, GROUPS, 2, 8, COLS),
            v(GROUPS, 2, HALVES, 2, 8, COLS),
            v(MEMBERS, (PICK_ROWS + 4) * COLS),
            v((PICK_ROWS + 4) * COLS, 128, dtype=BF16),
            v(n, rows, 128), v(n, rows, 128), v(rows, 128), v(geo.zl, rows, 128), v(2, rows, 128), v(2, rows, 128), v(rows, 128),
            v(n, rows, 128),
            dma((5,)), dma((2, 2, GROUPS)), dma((2, 2, GROUPS)), dma((2, 2, GROUPS)), dma((2, 5)),
        ],
        compiler_params=pltpu.CompilerParams(collective_id=0, has_side_effects=True, vmem_limit_bytes=40 * 2**20),
    )(x, obs_cell, obs_value, obs_variance, mask)
    out = pl.pallas_call(
        functools.partial(update_kernel, obs_cell.shape[1]),
        out_shape=jax.ShapeDtypeStruct((3, MEMBERS * ROWS, COLS), F32),
        in_specs=[vmem] * 3,
        out_specs=vmem,
        compiler_params=pltpu.CompilerParams(vmem_limit_bytes=32 * 2**20),
    )(f, c, y)
    return out.reshape(3, MEMBERS, ROWS, COLS)


def solution(mesh):
    geo = Geometry(mesh.shape["lon"], mesh.shape["lat"])
    in_specs = (P(None, None, "lat", "lon"), P(), P(), P(), P(None, None, ("lon", "lat")))
    out_specs = P(None, None, "lat", "lon")
    return jax.shard_map(
        functools.partial(body, geo), mesh=mesh, in_specs=in_specs, out_specs=out_specs, check_vma=False
    )
```

```python
import functools

import jax
import jax.numpy as jnp
from jax import lax
from jax.experimental import pallas as pl
from jax.experimental.pallas import tpu as pltpu
from jax.sharding import PartitionSpec as P

MESH = pl.DeviceIdType.MESH
F32 = jnp.float32
BF16 = jnp.bfloat16

STEPS = 4
LOC_RADIUS = 256
CORIOLIS = 0.1
SMALL_EPSILON = 1e-06
MEMBERS = 64
ROWS = 8
COLS = 128
GROUPS = 8
HALVES = 2 * STEPS
EXT = HALVES - 1
PICK_ROWS = ROWS + 2 * EXT


class Geometry:
    def __init__(self, n_lon, n_lat):
        self.n_lon, self.n_lat = n_lon, n_lat
        if (n_lon, n_lat) == (32, 32):
            self.x, self.y, self.zh, self.c = 4, 4, 4, 2
        else:
            self.x, self.y, self.zh, self.c = 1, 1, n_lat // 2, 2
        self.zl = n_lon // self.x
        self.near = self.x * self.y * self.c
        self.total_rows = ROWS * n_lat
        self.total_cols = COLS * n_lon

    def near_index(self, lon, lat):
        return (lon % self.x) * (self.y * self.c) + (lat // (self.zh * self.c)) * self.c + lat % self.c

    def near_peer(self, i, lon, lat):
        x, y, c = i // (self.y * self.c), (i // self.c) % self.y, i % self.c
        return (lon // self.x) * self.x + x, (y * self.zh + (lat // self.c) % self.zh) * self.c + c


def iota(shape, dim):
    return lax.broadcasted_iota(jnp.int32, shape, dim)


def roll(v, shift):
    return pltpu.roll(v, shift % COLS, 1)


def pack_edges(tiles):
    lane = iota((8, COLS), 1)
    out = None
    for s, t in enumerate(tiles):
        r = roll(t, 16 * s + 8)
        out = r if out is None else jnp.where(lane // 16 == s, r, out)
    return out


def unpack_edges(packed, s):
    return roll(packed, -(16 * s + 8))


def lon_diff(m, s, first, last):
    mp, sp, mm, sm = roll(m, -1), roll(s, -1), roll(m, 1), roll(s, 1)
    return (
        jnp.where(last, sp, mp) - jnp.where(first, sm, mm),
        jnp.where(last, mp, sp) - jnp.where(first, mm, sm),
    )


def column_of(row, eye):
    return jnp.sum(jnp.where(eye, row, 0.0), axis=1, keepdims=True)


class Sum:
    def __init__(self, geo, lon, lat, refs, sems):
        self.geo, self.lon, self.lat = geo, lon, lat
        self.src, self.near, self.mid, self.run, self.pair, self.pair_in, self.last, self.out = refs
        self.sems = sems
        self.me = geo.near_index(lon, lat)
        self.me_run = lon // geo.x

    def run_peer(self, i, lon, lat):
        return i * self.geo.x + lon % self.geo.x, lat

    def partner(self, step):
        geo, c = self.geo, self.geo.c
        zh = (self.lat // c) % geo.zh
        up = (zh + step) % 2 == 0
        other = jnp.where(up, zh + 1, zh + geo.zh - 1) % geo.zh
        return self.lon, ((self.lat // (geo.zh * c)) * geo.zh + other) * c + self.lat % c

    def _send(self, stage, src, dst, n, me, peer):
        def one(i, carry):
            p = lax.rem(me + i, n)
            pltpu.make_async_remote_copy(
                src_ref=src(p),
                dst_ref=dst.at[me],
                send_sem=self.sems.at[0, stage],
                recv_sem=self.sems.at[1, stage],
                device_id=peer(p, self.lon, self.lat),
                device_id_type=MESH,
            ).start()
            return carry

        lax.fori_loop(1, n, one, 0)

    def _wait(self, stage, buf, n, side=1):
        part = buf.at[pl.ds(0, n - 1)]
        pltpu.make_async_copy(part, part, self.sems.at[side, stage]).wait()

    def _added(self, buf, n):
        total = buf[0]
        for i in range(1, n):
            total = total + buf[i]
        return total

    def _pair_copy(self, step):
        return pltpu.make_async_remote_copy(
            src_ref=self.pair.at[step], dst_ref=self.pair_in.at[step], send_sem=self.sems.at[0, 2 + step],
            recv_sem=self.sems.at[1, 2 + step], device_id=self.partner(step), device_id_type=MESH,
        )

    def send_near(self):
        self.near[self.me] = self.src[self.me]
        self._send(0, lambda p: self.src.at[p], self.near, self.geo.near, self.me, self.geo.near_peer)

    def send_run(self):
        self._wait(0, self.near, self.geo.near)
        total = self._added(self.near, self.geo.near)
        self.mid[...] = total
        self.run[self.me_run] = total
        self._send(1, lambda p: self.mid, self.run, self.geo.zl, self.me_run, self.run_peer)

    def send_pair(self):
        self._wait(1, self.run, self.geo.zl)
        self.pair[0] = self._added(self.run, self.geo.zl)
        self._pair_copy(0).start()

    def send_pairs(self):
        self._pair_copy(0).wait_recv()
        self.pair[1] = self.pair[0] + self.pair_in[0]
        self._pair_copy(1).start()

    def send_last(self):
        self._pair_copy(1).wait_recv()
        total = self.pair[1] + self.pair_in[1]
        self.last[...] = total
        self.out[self.me] = total
        self._send(4, lambda p: self.last, self.out, self.geo.near, self.me, self.geo.near_peer)

    def wait_last(self):
        self._wait(4, self.out, self.geo.near)

    def wait_sends(self):
        for stage, buf, n in ((0, self.near, self.geo.near), (1, self.run, self.geo.zl), (4, self.out, self.geo.near)):
            self._wait(stage, buf, n, side=0)
        for step in range(2):
            self._pair_copy(step).wait_send()


def forecast_kernel(
    geo, x_hbm, cell_hbm, value_hbm, variance_hbm, mask_hbm,
    f_ref, c_ref, y_ref,
    x_ref, cell_ref, value_ref, variance_ref, mask_ref, main, side, edges, edges_in, series, series_in, late, late_in, ghosts, heights, onehot,
    s0, s1, s2, s3, s4, s5, s6, s7,
    in_sems, lon_sems, lat_sems, late_sems, sum_sems,
):
    lon, lat = lax.axis_index("lon"), lax.axis_index("lat")
    n_lon, n_lat = geo.n_lon, geo.n_lat
    east, west = lax.rem(lon + 1, n_lon), lax.rem(lon + n_lon - 1, n_lon)
    after, before = lax.rem(lat + 1, n_lat), lax.rem(lat + n_lat - 1, n_lat)
    shared = Sum(geo, lon, lat, (s0, s1, s2, s3, s4, s5, s6, s7), sum_sems)

    loads = [
        pltpu.make_async_copy(src, dst, in_sems.at[i])
        for i, (src, dst) in enumerate(
            (
                (x_hbm, x_ref), (cell_hbm, cell_ref), (value_hbm, value_ref), (variance_hbm, variance_ref), (mask_hbm, mask_ref),
            )
        )
    ]
    for load in loads:
        load.start()
    barrier = pltpu.get_barrier_semaphore()

    def greet(n, me, peer):
        def one(i, carry):
            pl.semaphore_signal(barrier, inc=1, device_id=peer(lax.rem(me + i, n), lon, lat), device_id_type=MESH)
            return carry

        lax.fori_loop(1, n, one, 0)

    for d in ((lon, after), (lon, before), shared.partner(0), shared.partner(1), (east, lat), (west, lat)):
        pl.semaphore_signal(barrier, inc=1, device_id=d, device_id_type=MESH)
    greet(geo.zl, shared.me_run, shared.run_peer)
    greet(geo.near, shared.me, geo.near_peer)

    row_first, col_first = lat * ROWS, lon * COLS
    lane = iota((8, COLS), 1)
    first, last = lane == 0, lane == COLS - 1
    edge = (lane < 8) | (lane >= COLS - 8)
    nothing = jnp.zeros((8, COLS), F32)
    has_before = jnp.where(lat > 0, 1.0, 0.0)
    has_after = jnp.where(lat < n_lat - 1, 1.0, 0.0)

    def field_row(f, g, r):
        return x_ref[f, pl.ds(g * 64 + r, 8, stride=8), :]

    def turning(r):
        row = (row_first + r).astype(F32)
        return CORIOLIS * ((2.0 * row + 1.0) / geo.total_rows - 1.0)

    def fit(r, v):
        return v * has_before if r < 0 else v * has_after if r >= ROWS else v

    class State:
        def __init__(self, g, own, sides):
            self.rows = [set(range(ROWS)) for _ in range(3)]
            for f in range(3):
                if sides:
                    packed = jnp.where(lane % 16 < 8, edges_in[0, g, f], edges_in[1, g, f])
                for r in range(ROWS):
                    main[f, r + 8] = field_row(f, g, r) if own else nothing
                    side[f, r + 8] = unpack_edges(packed, r) if sides else nothing

        def get(self, f, r):
            if r not in self.rows[f]:
                return None
            return main[f, r + 8], side[f, r + 8]

        def put(self, f, r, v):
            self.rows[f].add(r)
            main[f, r + 8], side[f, r + 8] = v

    def less(a, b):
        if a is None and b is None:
            return None
        if b is None:
            return a
        if a is None:
            return tuple(-q for q in b)
        return tuple(p - q for p, q in zip(a, b))

    def plus(a, b):
        if a is None or b is None:
            return a if b is None else b
        return tuple(p + q for p, q in zip(a, b))

    def scaled(a, k):
        return None if a is None else tuple(p * k for p in a)

    def lon_of(v):
        return None if v is None else lon_diff(v[0], v[1], first, last)

    def half_step(st, p, rows, ghost=None):
        at = (lambda f, r: ghost[r] if ghost is not None and r in ghost else st.get(f, r))
        for r in rows:
            if p % 2:
                slope = plus(lon_of(st.get(1, r)), less(at(2, r + 1), at(2, r - 1)))
                new = less(st.get(0, r), scaled(slope, 0.25))
                st.put(0, r, tuple(fit(r, v) for v in new))
            else:
                e, n, k = st.get(1, r), st.get(2, r), turning(r)
                new_e = less(plus(e, scaled(n, k)), scaled(lon_of(st.get(0, r)), 0.25))
                new_n = less(less(n, scaled(e, k)), scaled(less(at(0, r + 1), at(0, r - 1)), 0.25))
                if new_e is not None:
                    st.put(1, r, tuple(fit(r, v) for v in new_e))
                if new_n is not None:
                    st.put(2, r, tuple(fit(r, v) for v in new_n))

    beside = ((0, -1), (ROWS - 1, ROWS))

    def spread_tile(g, carry):
        for f in range(3):
            edges[g, f] = pack_edges([field_row(f, g, r) for r in range(ROWS)])
        st = State(g, True, False)
        sides = ([], [])
        for p in range(HALVES):
            if p > 0:
                half_step(st, p, range(-p, ROWS + p))
            f = 0 if p % 2 else 2
            for s, (r, outside) in enumerate(beside):
                m, e = st.get(f, r)
                series[s, g, p] = m
                sides[s].append(e)
                if p > 0:
                    ghosts[g, s, p, 0], ghosts[g, s, p, 1] = st.get(f, outside)
        for s in range(2):
            late[s, g, 0] = pack_edges(sides[s])
        here = pl.ds(pl.multiple_of(g * 8, 8), 8)
        for i in range(PICK_ROWS):
            heights[here, i * 128:(i + 1) * 128] = main[0, i - EXT + 8]
        for q in range(3):
            tiles = [side[0, i - EXT + 8] if i < PICK_ROWS else nothing for i in range(8 * q, 8 * q + 8)]
            heights[here, (PICK_ROWS + q) * 128:(PICK_ROWS + q + 1) * 128] = pack_edges(tiles)
        heights[here, (PICK_ROWS + 3) * 128:] = nothing
        return carry

    for load in loads:
        load.wait()
    lax.fori_loop(0, GROUPS, spread_tile, 0)

    big_row, big_col = iota((128, 128), 0), iota((128, 128), 1)
    eye = big_row == big_col
    cells = jnp.concatenate([cell_ref[0:1, :], cell_ref[1:2, :]], axis=1)
    obs_row, obs_col = cells // geo.total_cols, cells % geo.total_cols
    match_col = big_row + col_first == obs_col
    for i in range(PICK_ROWS):
        hit = match_col & (obs_row == row_first + (i - EXT))
        onehot[i * 128:(i + 1) * 128, :] = jnp.where(hit, 1.0, 0.0).astype(BF16)
    within = big_row % 16
    side_col = (jnp.where(within < 8, col_first - 8 + within, col_first + 120 + within) + geo.total_cols) % geo.total_cols
    match_col = side_col == obs_col
    for q in range(3):
        hit = match_col & (obs_row == row_first + (8 * q - EXT) + big_row // 16)
        i = PICK_ROWS + q
        onehot[i * 128:(i + 1) * 128, :] = jnp.where(hit, 1.0, 0.0).astype(BF16)
    onehot[(PICK_ROWS + 3) * 128:, :] = jnp.zeros((128, 128), BF16)
    total = jnp.zeros((3 * MEMBERS, 128), F32)
    for i in range((PICK_ROWS + 4) // 2):
        v = heights[:, i * 256:(i + 1) * 256]
        high = v.astype(BF16)
        rest = v - high.astype(F32)
        middle = rest.astype(BF16)
        low = (rest - middle.astype(F32)).astype(BF16)
        total = total + jnp.dot(
            jnp.concatenate([high, middle, low], axis=0), onehot[i * 256:(i + 1) * 256, :], preferred_element_type=F32
        )
    picked = total[:MEMBERS] + (total[MEMBERS:2 * MEMBERS] + total[2 * MEMBERS:])
    few, per = MEMBERS // geo.near, 128 // geo.near
    owned = jnp.where((obs_row // ROWS == lat) & (obs_col // COLS == lon), 1.0, 0.0)
    mask_row = jnp.concatenate([mask_ref[0], mask_ref[1]], axis=1).astype(F32)
    mask_col = column_of(mask_row, eye)
    share = mask_col * owned
    for i in range(geo.near):
        s0[i, 0:few, :] = picked[i * few:(i + 1) * few, :]
        s0[i, few:few + per, :] = share[i * per:(i + 1) * per, :]
        s0[i, few + per:, :] = jnp.zeros((s0.shape[1] - few - per, 128), F32)

    def lon_copies(g):
        return [
            pltpu.make_async_remote_copy(
                src_ref=edges.at[g], dst_ref=edges_in.at[s, g], send_sem=lon_sems.at[0, s, g], recv_sem=lon_sems.at[1, s, g],
                device_id=(d, lat), device_id_type=MESH,
            )
            for s, d in ((0, east), (1, west))
        ]

    def lat_copies(g, src, dst, sems):
        return [
            pltpu.make_async_remote_copy(
                src_ref=src.at[s, g], dst_ref=dst.at[1 - s, g], send_sem=sems.at[0, s, g],
                recv_sem=sems.at[1, 1 - s, g], device_id=(lon, d), device_id_type=MESH,
            )
            for s, d in ((0, before), (1, after))
        ]

    def series_copies(g):
        return lat_copies(g, series, series_in, lat_sems)

    def late_copies(g):
        return lat_copies(g, late, late_in, late_sems)

    def start(copies, lo, hi):
        def one(g, carry):
            for c in copies(g):
                c.start()
            return carry

        lax.fori_loop(lo, hi, one, 0)

    pl.semaphore_wait(barrier, 6 + (geo.zl - 1) + (geo.near - 1))
    shared.send_near()
    start(lon_copies, 0, GROUPS)
    start(series_copies, 0, 2)

    shared.send_run()
    start(series_copies, 2, 4)

    cells_col = column_of(cells.astype(F32), eye).astype(jnp.int32)
    row_col, col_col = cells_col // geo.total_cols, cells_col % geo.total_cols

    def damping(centre_row, centre_col):
        row_gap = row_col - centre_row
        col_gap = jnp.abs(col_col - centre_col)
        col_gap = jnp.minimum(col_gap, geo.total_cols - col_gap)
        distance = (row_gap * row_gap + col_gap * col_gap).astype(F32)
        return 1.0 + distance / (LOC_RADIUS * LOC_RADIUS)

    c_ref[0] = damping(obs_row // ROWS * ROWS + ROWS // 2, obs_col // COLS * COLS + COLS // 2)
    own = mask_col / damping(row_first + ROWS // 2, col_first + COLS // 2)
    value_col = column_of(jnp.concatenate([value_ref[0:1, :], value_ref[1:2, :]], axis=1), eye)
    variance_col = column_of(jnp.concatenate([variance_ref[0:1, :], variance_ref[1:2, :]], axis=1), eye)
    c_ref[1] = jnp.broadcast_to(1.0 / variance_col, (128, 128))
    c_ref[2] = jnp.broadcast_to(value_col, (128, 128))
    c_ref[3] = jnp.broadcast_to(own, (128, 128))

    def spread_sides(g, carry):
        for c in lon_copies(g):
            c.wait_recv()
        st = State(g, False, True)
        sides, mains = ([], []), ([], [])
        for p in range(HALVES):
            if p > 0:
                reach = EXT - p
                rows = [
                    r for r in range(-p, ROWS + p)
                    if -1 - reach <= r <= reach or ROWS - 1 - reach <= r <= ROWS + reach
                ]
                half_step(st, p, rows)
            f = 0 if p % 2 else 2
            for s, (r, outside) in enumerate(beside):
                m, e = st.get(f, r)
                mains[s].append(m)
                sides[s].append(e)
                if p > 0:
                    m, e = st.get(f, outside)
                    ghosts[g, s, p, 0] += m
                    ghosts[g, s, p, 1] += e
        for s in range(2):
            late[s, g, 0] += pack_edges(sides[s])
            late[s, g, 1] = pack_edges(mains[s])
        return carry

    def settle(g, carry):
        for c in series_copies(g) + late_copies(g):
            c.wait_recv()
        st = State(g, True, True)
        packed = [(late_in[s, g, 0], late_in[s, g, 1]) for s in range(2)]
        for p in range(1, HALVES + 1):
            ghost = {}
            for s, ((_, outside), there) in enumerate(zip(beside, (has_before, has_after))):
                m = series_in[s, g, p - 1] + jnp.where(edge, unpack_edges(packed[s][1], p - 1), 0.0)
                v = (m * there, unpack_edges(packed[s][0], p - 1) * there)
                if p > 1:
                    v = plus(v, (ghosts[g, s, p - 1, 0], ghosts[g, s, p - 1, 1]))
                ghost[outside] = v
            half_step(st, p, range(ROWS), ghost)
        for f in range(3):
            for r in range(ROWS):
                f_ref[f * ROWS + r, pl.ds(pl.multiple_of(g * 8, 8), 8), :] = main[f, r + 8]
        return carry

    lax.fori_loop(0, 5, spread_sides, 0)
    shared.send_pair()
    start(series_copies, 4, 6)
    lax.fori_loop(5, GROUPS, spread_sides, 0)
    start(late_copies, 0, 4)
    shared.send_pairs()
    start(series_copies, 6, GROUPS)
    start(late_copies, 4, GROUPS)
    lax.fori_loop(0, 2, settle, 0)
    shared.send_last()

    lax.fori_loop(2, GROUPS, settle, 0)
    shared.wait_last()
    for i in range(geo.near):
        y_ref[i * few:(i + 1) * few, :] = s7[i, 0:few, :]
        here = slice(i * per, (i + 1) * per)
        c_ref[0, here, :] = s7[i, few:few + per, :] / c_ref[0, here, :]
    weighted = c_ref[0]
    following = jnp.sum(jnp.where(big_col == big_row + 1, weighted, 0.0), axis=1, keepdims=True)
    c_ref[4] = jnp.broadcast_to(following, (128, 128))

    shared.wait_sends()

    def finish(g, carry):
        for c in lon_copies(g) + series_copies(g) + late_copies(g):
            c.wait_send()
        return carry

    lax.fori_loop(0, GROUPS, finish, 0)


def added_sublanes(v):
    t = v.reshape(8, 8, COLS).sum(axis=0)
    for s in (4, 2, 1):
        t = t + pltpu.roll(t, s, 0)
    return t


def tall(v):
    return jnp.concatenate([v] * 8, axis=0)


def across(column):
    return jnp.broadcast_to(column, (column.shape[0], COLS))


def update_kernel(n_obs, f_ref, c_ref, y_ref, out_ref):
    y = y_ref[...]
    mean = added_sublanes(y) * (1.0 / MEMBERS)
    b = y - tall(mean)
    a = jnp.where(iota((MEMBERS, COLS), 0) == iota((MEMBERS, COLS), 1), 1.0, 0.0)
    a_mean = jnp.zeros((8, COLS), F32)
    left = iota((8, COLS), 1) < MEMBERS

    def row(i, k):
        return jnp.broadcast_to(c_ref[i, k:k + 1, :], (8, COLS))

    d, m = across(b[:, 0:1]), across(mean[:, 0:1])
    for k in range(2 * n_obs):
        if k == n_obs:
            a, a_mean = jnp.where(tall(left), a, b), jnp.where(left, a_mean, mean)
        later = k >= n_obs
        obs, obs_mean = (a, a_mean) if later else (b, mean)
        if k + 1 < 2 * n_obs:
            d_next, m_next = across(obs[:, k + 1:k + 2]), across(obs_mean[:, k + 1:k + 2])
        s = added_sublanes(d * d) * (1.0 / (MEMBERS - 1)) + SMALL_EPSILON
        ratio = s * row(1, k)
        root = lax.rsqrt(1.0 + ratio)
        gain = root - 1.0
        shift = ratio * (root * root) * (row(2, k) - m)
        scale = 1.0 / ((MEMBERS - 1) * s)
        if k + 1 < 2 * n_obs:
            c = row(4, k) * scale * added_sublanes(d_next * d)
            new_d, new_m = d_next + tall(c * gain) * d, m_next + c * shift
        link, own = row(0, k), row(3, k)
        c = (jnp.where(left, own, link) if later else own) * scale * added_sublanes(a * d)
        a, a_mean = a + tall(c * gain) * d, a_mean + c * shift
        if not later:
            c = link * scale * added_sublanes(b * d)
            b, mean = b + tall(c * gain) * d, mean + c * shift
        if k + 1 < 2 * n_obs:
            d, m = new_d, new_m
    t = (a + tall(a_mean))[:, :MEMBERS]
    t_high = t.astype(BF16)
    t_low = (t - t_high.astype(F32)).astype(BF16)
    lhs = jnp.concatenate([t_high, t_high, t_low, t_low], axis=1)
    for i in range(0, 3 * ROWS, 2):
        v = jnp.concatenate([f_ref[i], f_ref[i + 1]], axis=1)
        high = v.astype(BF16)
        low = (v - high.astype(F32)).astype(BF16)
        r = jnp.dot(lhs, jnp.concatenate([high, low, high, low], axis=0), preferred_element_type=F32)
        for q in range(2):
            out_ref[(i + q) // ROWS, pl.ds((i + q) % ROWS, MEMBERS, stride=ROWS), :] = r[:, q * COLS:(q + 1) * COLS]


def body(geo, model_variables, obs_cell, obs_value, obs_variance, tile_mask):
    vmem = pl.BlockSpec(memory_space=pltpu.VMEM)
    x = model_variables.reshape(3, MEMBERS * ROWS, COLS)
    mask = jnp.transpose(tile_mask, (0, 2, 1))
    n, rows = geo.near, -(-(MEMBERS + 128) // geo.near // 8) * 8
    dma = pltpu.SemaphoreType.DMA

    def v(*shape, dtype=F32):
        return pltpu.VMEM(shape, dtype)

    f, c, y = pl.pallas_call(
        functools.partial(forecast_kernel, geo),
        out_shape=(
            jax.ShapeDtypeStruct((3 * ROWS, MEMBERS, COLS), F32),
            jax.ShapeDtypeStruct((5, 128, 128), F32),
            jax.ShapeDtypeStruct((MEMBERS, 128), F32),
        ),
        in_specs=[pl.BlockSpec(memory_space=pltpu.HBM)] * 5,
        out_specs=(vmem, vmem, vmem),
        scratch_shapes=[
            v(3, MEMBERS * ROWS, COLS),
            v(*obs_cell.shape, dtype=jnp.int32), v(*obs_value.shape), v(*obs_value.shape), v(*mask.shape, dtype=jnp.int32),
            v(3, 24, 8, COLS),
            v(3, 24, 8, COLS),
            v(GROUPS, 3, 8, COLS),
            v(2, GROUPS, 3, 8, COLS),
            v(2, GROUPS, HALVES, 8, COLS),
            v(2, GROUPS, HALVES, 8, COLS),
            v(2, GROUPS, 2, 8, COLS),
            v(2, GROUPS, 2, 8, COLS),
            v(GROUPS, 2, HALVES, 2, 8, COLS),
            v(MEMBERS, (PICK_ROWS + 4) * COLS),
            v((PICK_ROWS + 4) * COLS, 128, dtype=BF16),
            v(n, rows, 128), v(n, rows, 128), v(rows, 128), v(geo.zl, rows, 128), v(2, rows, 128), v(2, rows, 128), v(rows, 128),
            v(n, rows, 128),
            dma((5,)), dma((2, 2, GROUPS)), dma((2, 2, GROUPS)), dma((2, 2, GROUPS)), dma((2, 5)),
        ],
        compiler_params=pltpu.CompilerParams(collective_id=0, has_side_effects=True, vmem_limit_bytes=40 * 2**20),
    )(x, obs_cell, obs_value, obs_variance, mask)
    out = pl.pallas_call(
        functools.partial(update_kernel, obs_cell.shape[1]),
        out_shape=jax.ShapeDtypeStruct((3, MEMBERS * ROWS, COLS), F32),
        in_specs=[vmem] * 3,
        out_specs=vmem,
        compiler_params=pltpu.CompilerParams(vmem_limit_bytes=32 * 2**20),
    )(f, c, y)
    return out.reshape(3, MEMBERS, ROWS, COLS)


def solution(mesh):
    geo = Geometry(mesh.shape["lon"], mesh.shape["lat"])
    in_specs = (P(None, None, "lat", "lon"), P(), P(), P(), P(None, None, ("lon", "lat")))
    out_specs = P(None, None, "lat", "lon")
    return jax.shard_map(
        functools.partial(body, geo), mesh=mesh, in_specs=in_specs, out_specs=out_specs, check_vma=False
    )
```
